512 devices in a mesh: lat: 64 (over z, x, core), fld: 8 (over y).
Axes of the slice: x: 4, y: 8, z: 8, core: 2. Of those that a mesh axis runs over, the one named last changes fastest.
Arguments:
- grid: float32 [2, 640, 32, 2688], P(None, 'lat', 'fld'), may hold values from -6 to 6
- row_points: int32 [640], P('lat'), may hold values from 20 to 2576, as said below
- assignment: int32 [640], replicated, may hold values from 0 to 639, each once
- legendre: float32 [640, 640, 640], P('lat', 'fld'), may hold values from -0.25 to 0.25
- gauss_weights: float32 [640], P('fld'), may hold values from 0.25 to 2
- to_modes: float32 [32, 32], replicated, may hold values from -1 to 1
- from_modes: float32 [32, 32], replicated, may hold values from -1 to 1
- mode_depths: float32 [32], replicated, may hold values from 0.5 to 8
Outputs:
- grid_next: float32 [2, 640, 32, 2688], P(None, 'lat', 'fld')
The draws below stay inside these ranges and needn't reach their ends.
Inputs may be any that keep to these rules, and one draw needn't show every extreme that they name: `row_points`: multiples of 4; row j, counted from the pole, has between 20 + 4 j - 12 and 20 + 4 j + 12 points, the row beside the equator exactly 2576; both hemispheres alike. `assignment`: every wavenumber from 0 to 639 stands in exactly one slot.
All inputs are finite; a program needn't handle non-finite values.
Results may differ from the reference program's by a relative error of at most 0.0003.
Values sent between devices are 32-bit elements; how exact they have to be, the bound alone decides.
No kernel may reach another device: no remote copies, remote signals or barrier semaphores. Data moves between devices by JAX's collectives and lax.ppermute only.
A program may use at most 128 MiB of HBM per device.

```python
import math
import jax
import jax.numpy as jnp
from jax import lax

HALF = 640
MTRUNC = 640
LON = 2688
FL = 32


def draw_row_points(key, part):
    key = jax.random.fold_in(key, 11)
    position = jnp.arange(HALF, dtype=jnp.int32)
    jitter = jax.random.randint(key, (HALF,), -3, 4, dtype=jnp.int32)
    quarters = jnp.clip(5 + position + jitter, 5, HALF + 4)
    quarters = jnp.where(position == HALF - 1, HALF + 4, quarters)
    return (4 * quarters).astype(jnp.int32)


def level_of(rng, dims, shards, low, high):
    def one(dim, parts):
        steps = jax.random.uniform(jax.random.fold_in(jax.random.fold_in(rng, 6), dim), (parts,), jnp.float32, low / len(shards), high / len(shards))
        return jnp.repeat(jnp.exp(steps), dims[dim] // parts).reshape((-1,) + (1,) * (len(dims) - dim - 1))

    factor_of = one(*shards[0])
    for cut in shards[1:]:
        factor_of = factor_of * one(*cut)
    return factor_of


def centred(stream_key, extent, spread, reach, cuts=(), kind=jnp.bfloat16):
    factor_of = level_of(stream_key, extent, cuts, -0.22, 0.18) if cuts else 1.0
    values = jax.random.normal(stream_key, extent, jnp.float32) * spread * factor_of
    return jnp.minimum(jnp.maximum(values, -reach), reach).astype(kind)


def setup_inputs(seed: int = 0) -> dict:
    arg_keys = jax.random.split(jax.random.key(seed), 9)
    return {
        "grid": centred(arg_keys[0], (2, HALF, FL, LON), 1.0, 6.0, ((1, 64), (2, 8)), jnp.float32),
        "row_points": draw_row_points(jax.random.fold_in(arg_keys[8], 71), 0),
        "assignment": jax.random.permutation(arg_keys[2], MTRUNC).astype(jnp.int32),
        "legendre": centred(arg_keys[3], (MTRUNC, HALF, MTRUNC), HALF ** -0.5, 0.25, ((0, 64), (1, 8)), jnp.float32),
        "gauss_weights": jnp.clip(jnp.exp(math.log(2.0) - 2.0794415 * jax.random.uniform(arg_keys[4], (HALF,), jnp.float32) ** level_of(arg_keys[4], (HALF,), ((0, 8),), -0.2, 0.2)), 0.25, 2.0),
        "to_modes": centred(arg_keys[5], (FL, FL), FL ** -0.5, 1.0, (), jnp.float32),
        "from_modes": centred(arg_keys[6], (FL, FL), FL ** -0.5, 1.0, (), jnp.float32),
        "mode_depths": jnp.clip(jnp.exp(jax.random.uniform(arg_keys[7], (FL,), jnp.float32, math.log(0.5), math.log(8.0))), 0.5, 8.0),
    }


PRECISE = lax.Precision.HIGHEST


def twiddle_tables(point_count, wavenumbers, blocks):
    inner_index = jnp.arange(128, dtype=jnp.int32)
    outer_index = jnp.arange(blocks, dtype=jnp.int32) * 128
    phase_step = (2.0 * math.pi) / point_count.astype(jnp.float32)
    inner_phase = ((inner_index[:, None] * wavenumbers[None, :]) % point_count).astype(jnp.float32) * phase_step
    outer_phase = ((outer_index[:, None] * wavenumbers[None, :]) % point_count).astype(jnp.float32) * phase_step
    return jnp.cos(inner_phase), jnp.sin(inner_phase), jnp.cos(outer_phase), jnp.sin(outer_phase)


def forward_row(row_values, point_count, wavenumbers):
    lon_points = row_values.shape[-1]
    blocks = lon_points // 128
    cos_in, sin_in, cos_out, sin_out = twiddle_tables(point_count, wavenumbers, blocks)
    column = jnp.arange(lon_points, dtype=jnp.int32)
    row_values = jnp.where(column < point_count, row_values, 0.0)
    blocked = row_values.reshape(row_values.shape[0], row_values.shape[1], blocks, 128)
    part_re = jnp.einsum("hfab,bm->hfam", blocked, cos_in, precision=PRECISE)
    part_im = -jnp.einsum("hfab,bm->hfam", blocked, sin_in, precision=PRECISE)
    real_part = jnp.sum(part_re * cos_out + part_im * sin_out, axis=2)
    imag_part = jnp.sum(part_im * cos_out - part_re * sin_out, axis=2)
    scaling = jnp.where(2 * wavenumbers < point_count, 1.0 / point_count.astype(jnp.float32), 0.0)
    return jnp.stack([real_part, imag_part], axis=2) * scaling


def inverse_row(coeffs, point_count, wavenumbers, lon_points):
    blocks = lon_points // 128
    cos_in, sin_in, cos_out, sin_out = twiddle_tables(point_count, wavenumbers, blocks)
    weighting = jnp.where(2 * wavenumbers < point_count, jnp.where(wavenumbers == 0, 1.0, 2.0), 0.0)
    real_part = coeffs[:, :, 0] * weighting
    imag_part = coeffs[:, :, 1] * weighting
    turned_re = real_part[:, :, None, :] * cos_out - imag_part[:, :, None, :] * sin_out
    turned_im = real_part[:, :, None, :] * sin_out + imag_part[:, :, None, :] * cos_out
    values = jnp.einsum("hfam,bm->hfab", turned_re, cos_in, precision=PRECISE) - jnp.einsum("hfam,bm->hfab", turned_im, sin_in, precision=PRECISE)
    values = values.reshape(values.shape[0], values.shape[1], lon_points)
    column = jnp.arange(lon_points, dtype=jnp.int32)
    return jnp.where(column < point_count, values, 0.0)


def reference(grid, row_points, assignment, legendre, gauss_weights, to_modes, from_modes, mode_depths):
    lon_points = grid.shape[-1]
    slot_total = assignment.shape[0]

    def forward_one(row_index):
        return forward_row(grid[:, row_index], row_points[row_index], assignment)

    fourier = lax.map(forward_one, jnp.arange(grid.shape[1], dtype=jnp.int32))
    weighted = jnp.moveaxis(fourier, -1, 0) * gauss_weights[None, :, None, None, None]
    degree = jnp.arange(slot_total, dtype=jnp.int32)
    parity_sign = jnp.where(degree % 2 == 0, 1.0, -1.0)

    def spectrum_one(slot_index):
        legendre_rows = legendre[slot_index]
        slot_data = weighted[slot_index]
        northern = jnp.einsum("jk,jfr->kfr", legendre_rows, slot_data[:, 0], precision=PRECISE)
        southern = jnp.einsum("jk,jfr->kfr", legendre_rows, slot_data[:, 1], precision=PRECISE)
        wave_degree = assignment[slot_index] + degree
        within = wave_degree < slot_total
        combined = (northern + parity_sign[:, None, None] * southern) * within[:, None, None]
        factor = 1.0 + mode_depths[None, :] * (wave_degree * (wave_degree + 1)).astype(jnp.float32)[:, None] / (slot_total * (slot_total + 1))
        in_modes = jnp.einsum("gf,kfr->kgr", to_modes, combined, precision=PRECISE) / factor[:, :, None]
        updated = jnp.einsum("gf,kfr->kgr", from_modes, in_modes, precision=PRECISE)
        back_north = jnp.einsum("jk,kfr->jfr", legendre_rows, updated, precision=PRECISE)
        back_south = jnp.einsum("jk,kfr->jfr", legendre_rows, updated * parity_sign[:, None, None], precision=PRECISE)
        return jnp.stack([back_north, back_south], axis=1)

    synthesis = lax.map(spectrum_one, jnp.arange(slot_total, dtype=jnp.int32))
    synthesis = jnp.moveaxis(synthesis, 0, -1)

    def inverse_one(row_index):
        return inverse_row(synthesis[row_index], row_points[row_index], assignment, lon_points)

    result = lax.map(inverse_one, jnp.arange(grid.shape[1], dtype=jnp.int32))
    return jnp.moveaxis(result, 0, 1)
```

```python
import math

import numpy as np
import jax
import jax.numpy as jnp
from jax import lax
from jax.experimental import pallas as pl
from jax.experimental.pallas import tpu as pltpu
from jax.sharding import PartitionSpec as P

F32 = jnp.float32
BF16 = jnp.bfloat16

HEMI = 2
ROWS = 10
FIELDS = 4
LEVELS = 32
LON = 2688
BLOCKS = LON // 128
WAVES = 640
LAT = 64
FLD = 8
PART = 2 * HEMI * FIELDS
MSG = ROWS * PART
LANES = 384
QUARTER = WAVES // 4
LEG = 896
VMEM = 48 << 20


def halves(x):
    top = x.astype(BF16)
    return top, (x - top.astype(F32)).astype(BF16)


def dot_split(a, b, dims):
    (ah, al), (bh, bl) = a, b
    d = (dims, ((), ()))
    out = lax.dot_general(ah, bl, d, preferred_element_type=F32)
    out = out + lax.dot_general(al, bh, d, preferred_element_type=F32)
    return out + lax.dot_general(ah, bh, d, preferred_element_type=F32)


AB = ((1,), (0,))
ABT = ((1,), (1,))


def turn(waves, points, index):
    product = waves * index
    quarter = points * 0.25
    count = jnp.floor(product * (4.0 / points) + 0.5)
    angle = (product - count * quarter) * (2.0 * math.pi / points)
    z = angle * angle
    s = angle * (
        1.0 + z * (-1 / 6 + z * (1 / 120 + z * (-1 / 5040 + z * (1 / 362880))))
    )
    c = 1.0 + z * (-0.5 + z * (1 / 24 + z * (-1 / 720 + z * (1 / 40320 - z / 3628800))))
    quad = count.astype(jnp.int32) & 3
    odd = (quad & 1) == 1
    cos_v = jnp.where(odd, s, c)
    sin_v = jnp.where(odd, c, s)
    cos_v = jnp.where((quad == 1) | (quad == 2), -cos_v, cos_v)
    sin_v = jnp.where(quad >= 2, -sin_v, sin_v)
    return cos_v, sin_v


def iota(shape, dim):
    return lax.broadcasted_iota(jnp.int32, shape, dim).astype(F32)


def tables(waves, points, cs_ref):
    c0, s0 = turn(waves, points, iota((16, WAVES), 0))
    c1, s1 = turn(waves, points, iota((8, WAVES), 0) * 16.0)
    for b in range(8):
        cb, sb = c1[b : b + 1], s1[b : b + 1]
        cs_ref[16 * b : 16 * b + 16, :WAVES] = c0 * cb - s0 * sb
        cs_ref[16 * b : 16 * b + 16, WAVES:] = s0 * cb + c0 * sb
    return turn(waves, points, iota((24, WAVES), 0) * 128.0)


def forward_kernel(points_ref, waves_ref, grid_ref, out_ref, cs_ref, fourier_ref):
    r = pl.program_id(0)
    count = points_ref[r]
    points = jnp.full((1, WAVES), count, jnp.int32).astype(F32)
    waves = waves_ref[...]
    co, so = tables(waves, points, cs_ref)
    wh, wl = halves(cs_ref[...])
    x = jnp.concatenate([grid_ref[0, 0], grid_ref[1, 0]], axis=0)
    column = lax.broadcasted_iota(jnp.int32, x.shape, 1)
    x = jnp.where(column < count, x, 0.0)
    x = jnp.concatenate([x[:, 128 * a : 128 * a + 128] for a in range(BLOCKS)], axis=0)
    xh, xl = halves(x)
    d = (AB, ((), ()))
    part = lax.dot_general(
        jnp.concatenate([xh, xl], axis=1),
        jnp.concatenate([wh, wh], axis=0),
        d,
        preferred_element_type=F32,
    ) + lax.dot_general(xh, wl, d, preferred_element_type=F32)
    re = jnp.zeros((8, WAVES), F32)
    im = jnp.zeros((8, WAVES), F32)
    for a in range(BLOCKS):
        pc = part[8 * a : 8 * a + 8, :WAVES]
        ps = part[8 * a : 8 * a + 8, WAVES:]
        ca, sa = co[a : a + 1], so[a : a + 1]
        re = re + (pc * ca - ps * sa)
        im = im - (ps * ca + pc * sa)
    scale = jnp.where(2.0 * waves < points, 1.0 / points, 0.0)
    row = pl.multiple_of(r * PART, PART)
    fourier_ref[pl.ds(row, 8), :] = re * scale
    fourier_ref[pl.ds(row + 8, 8), :] = im * scale

    @pl.when(r == ROWS - 1)
    def _():
        y = fourier_ref[...]
        shared = []
        for q in range(2):
            piece = y[:, 512 + 64 * q : 576 + 64 * q]
            shared += [jnp.concatenate([piece, piece], axis=1)] * 2
        full = jnp.concatenate(
            [
                y[:, :512],
                jnp.concatenate(shared, axis=1),
                jnp.zeros((LANES - 2 * MSG, 512), F32),
            ],
            axis=0,
        )
        out_ref[...] = full.T


def forward(row_points, waves, grid):
    return pl.pallas_call(
        forward_kernel,
        grid=(ROWS,),
        in_specs=[
            pl.BlockSpec(memory_space=pltpu.SMEM),
            pl.BlockSpec((1, WAVES), lambda r: (0, 0)),
            pl.BlockSpec((HEMI, 1, FIELDS, LON), lambda r: (0, r, 0, 0)),
        ],
        out_specs=pl.BlockSpec((LAT * FLD, LANES), lambda r: (0, 0)),
        out_shape=jax.ShapeDtypeStruct((LAT * FLD, LANES), F32),
        scratch_shapes=[
            pltpu.VMEM((128, 2 * WAVES), F32),
            pltpu.VMEM((MSG, WAVES), F32),
        ],
        compiler_params=pltpu.CompilerParams(vmem_limit_bytes=VMEM),
        cost_estimate=pl.CostEstimate(
            flops=3_000_000_000, bytes_accessed=2_000_000, transcendentals=0
        ),
        name="forward_fourier",
    )(row_points, waves, grid)


def inverse_kernel(points_ref, waves_ref, coeff_ref, out_ref, cs_ref, fourier_ref):
    r = pl.program_id(0)

    @pl.when(r == 0)
    def _():
        t = coeff_ref[...].T
        fourier_ref[:, :512] = t[:MSG]
        lane = lax.broadcasted_iota(jnp.int32, (MSG, 128), 1)
        sums = []
        for q in range(2):
            s = t[MSG : 2 * MSG, 256 * q : 256 * q + 128]
            s = s + t[MSG : 2 * MSG, 256 * q + 128 : 256 * q + 256]
            sums.append(s + pltpu.roll(s, 64, 1))
        fourier_ref[:, 512:] = jnp.where(lane < 64, sums[0], sums[1])

    count = points_ref[r]
    points = jnp.full((1, WAVES), count, jnp.int32).astype(F32)
    waves = waves_ref[...]
    co, so = tables(waves, points, cs_ref)
    wh, wl = halves(cs_ref[...])
    weight = jnp.where(2.0 * waves < points, jnp.where(waves == 0.0, 1.0, 2.0), 0.0)
    row = pl.multiple_of(r * PART, PART)
    re = fourier_ref[pl.ds(row, 8), :] * weight
    im = fourier_ref[pl.ds(row + 8, 8), :] * weight
    cosine, sine = [], []
    for a in range(BLOCKS):
        ca, sa = co[a : a + 1], so[a : a + 1]
        cosine.append(re * ca - im * sa)
        sine.append(-(re * sa + im * ca))
    turned = jnp.concatenate(
        [jnp.concatenate(cosine, axis=0), jnp.concatenate(sine, axis=0)], axis=1
    )
    th, tl = halves(turned)
    d = (ABT, ((), ()))
    both = lax.dot_general(
        th, jnp.concatenate([wh, wl], axis=0), d, preferred_element_type=F32
    )
    values = both[:, :128] + both[:, 128:]
    values = values + lax.dot_general(tl, wh, d, preferred_element_type=F32)
    wide = jnp.concatenate(
        [values[8 * a : 8 * a + 8] for a in range(BLOCKS)], axis=1
    )
    column = lax.broadcasted_iota(jnp.int32, wide.shape, 1)
    wide = jnp.where(column < count, wide, 0.0)
    out_ref[0, 0] = wide[:FIELDS]
    out_ref[1, 0] = wide[FIELDS:]


def inverse(row_points, waves, coeffs):
    return pl.pallas_call(
        inverse_kernel,
        grid=(ROWS,),
        in_specs=[
            pl.BlockSpec(memory_space=pltpu.SMEM),
            pl.BlockSpec((1, WAVES), lambda r: (0, 0)),
            pl.BlockSpec((LAT * FLD, LANES), lambda r: (0, 0)),
        ],
        out_specs=pl.BlockSpec((HEMI, 1, FIELDS, LON), lambda r: (0, r, 0, 0)),
        out_shape=jax.ShapeDtypeStruct((HEMI, ROWS, FIELDS, LON), F32),
        scratch_shapes=[
            pltpu.VMEM((128, 2 * WAVES), F32),
            pltpu.VMEM((MSG, WAVES), F32),
        ],
        compiler_params=pltpu.CompilerParams(vmem_limit_bytes=VMEM),
        name="inverse_fourier",
    )(row_points, waves, coeffs)


def pack_kernel(me_ref, legendre_ref, weight_ref, *refs):
    out_refs, tile_ref = refs[:FLD], refs[FLD]
    me = me_ref[0]
    lane = lax.broadcasted_iota(jnp.int32, (FLD * ROWS, LEG - WAVES), 1)
    weight = weight_ref[...]
    for t in range(FLD):
        g = lax.rem(me + t, FLD)
        shared = FLD + g // 4
        shift = lax.rem(WAVES - QUARTER * lax.rem(g, 4), WAVES)
        quarter = pltpu.roll(legendre_ref[shared], shift, 1)[:, : LEG - WAVES]
        extra = jnp.where(lane == QUARTER, weight, 0.0)
        quarter = jnp.where(lane < QUARTER, quarter, extra)
        own = legendre_ref[g]
        for i in range(LEG // 128):
            cut = slice(128 * i, 128 * i + 128)
            tile_ref[t, i] = own[:, cut] if i < 5 else quarter[:, 128 * i - WAVES :][:, :128]
        for i in range(LEG // 128):
            for r in range(ROWS):
                rows = pl.ds(r, FLD, stride=ROWS)
                out_refs[t][FLD * r : FLD * r + FLD, 128 * i : 128 * i + 128] = tile_ref[
                    t, i, rows, :
                ]


def pack(me, legendre, gauss_weights):
    vmem = pl.BlockSpec(memory_space=pltpu.VMEM)
    return pl.pallas_call(
        pack_kernel,
        in_specs=[pl.BlockSpec(memory_space=pltpu.SMEM), vmem, vmem],
        out_specs=[vmem] * FLD,
        out_shape=[jax.ShapeDtypeStruct((FLD * ROWS, LEG), F32)] * FLD,
        scratch_shapes=[pltpu.VMEM((FLD, LEG // 128, FLD * ROWS, 128), F32)],
        compiler_params=pltpu.CompilerParams(vmem_limit_bytes=VMEM),
        name="pack_legendre",
    )(me, legendre, gauss_weights.reshape(FLD * ROWS, 1))


def legendre_kernel(
    me_ref, assignment_ref, coeff_ref, to_ref, from_ref, depth_ref, *refs
):
    blocks, (out_ref, leg_ref, a_ref, x_ref, y_ref) = refs[:FLD], refs[FLD:]
    lat, fld = me_ref[1], me_ref[0]
    for t in range(FLD):
        source = lax.rem(fld + FLD - t, FLD)
        for r in range(ROWS):
            place = pl.multiple_of(r * LAT + FLD * source, FLD)
            leg_ref[pl.ds(place, FLD), :] = blocks[t][FLD * r : FLD * r + FLD, :]
    weight = leg_ref[:, LEG - 128 :].T[QUARTER - 128 : QUARTER - 127, :]
    lh, ll = halves(leg_ref[...])

    t = coeff_ref[...].T
    for kind, dest in ((0, a_ref), (1, x_ref)):
        for u in range(ROWS // 2):
            row = kind * MSG + 2 * u * PART
            even, odd = t[row : row + PART], t[row + PART : row + 2 * PART]
            for g in range(FLD):
                cut = slice(LAT * g, LAT * g + LAT)
                dest[PART * g : PART * g + PART, 128 * u : 128 * u + 128] = (
                    jnp.concatenate([even[:, cut], odd[:, cut]], axis=1)
                )
    own = halves(a_ref[...] * weight)
    shared = halves(x_ref[...] * weight)
    spectrum = jnp.concatenate(
        [
            dot_split(own, (lh[:, :WAVES], ll[:, :WAVES]), AB),
            dot_split(shared, (lh[:, WAVES:], ll[:, WAVES:]), AB),
        ],
        axis=1,
    )

    modes = dot_split(halves(to_ref[...]), halves(spectrum), AB)
    lane = lax.broadcasted_iota(jnp.int32, (1, LEG), 1)
    is_own = lane < WAVES
    degree = jnp.where(is_own, lane, lane - WAVES + QUARTER * lax.rem(fld, 4))
    wave_own = assignment_ref[lat * ROWS + fld]
    wave_shared = assignment_ref[lat * ROWS + FLD + fld // 4]
    total = degree + jnp.where(is_own, wave_own, wave_shared)
    within = (total < WAVES) & (lane < WAVES + QUARTER)
    total = jnp.where(within, total, 0)
    sign = jnp.where((degree & 1) == 0, 1.0, -1.0)
    ratio = (total * (total + 1)).astype(F32) * (1.0 / (WAVES * (WAVES + 1)))
    half = 2 * LEVELS
    modes = modes[:half] + sign * modes[half:]
    modes = jnp.where(within, modes, 0.0) / (1.0 + depth_ref[...] * ratio)
    updated = dot_split(halves(from_ref[...]), halves(modes), AB)
    row_id = lax.broadcasted_iota(jnp.int32, updated.shape, 0)
    updated = jnp.where((row_id & FIELDS) == 0, updated, updated * sign)

    for kind, cols in ((0, slice(0, WAVES)), (1, slice(WAVES, LEG))):
        back = dot_split(halves(updated[:, cols]), (lh[:, cols], ll[:, cols]), ABT)
        for u in range(ROWS // 2):
            row = kind * MSG + 2 * u * PART
            for g in range(0, FLD, 2):
                one = back[PART * g : PART * g + PART, 128 * u : 128 * u + 128]
                two = back[PART * g + PART : PART * g + 2 * PART, 128 * u : 128 * u + 128]
                for odd in range(2):
                    cut = slice(64 * odd, 64 * odd + 64)
                    y_ref[
                        row + PART * odd : row + PART * odd + PART, LAT * g : LAT * g + 128
                    ] = jnp.concatenate([one[:, cut], two[:, cut]], axis=1)
    y_ref[2 * MSG :, :] = jnp.zeros((LANES - 2 * MSG, LAT * FLD), F32)
    out_ref[...] = y_ref[...].T


def legendre_round(me, assignment, coeffs, to_big, from_big, depth_big, blocks):
    smem = pl.BlockSpec(memory_space=pltpu.SMEM)
    vmem = pl.BlockSpec(memory_space=pltpu.VMEM)
    return pl.pallas_call(
        legendre_kernel,
        in_specs=[smem, smem] + [vmem] * (4 + FLD),
        out_specs=vmem,
        out_shape=jax.ShapeDtypeStruct((LAT * FLD, LANES), F32),
        scratch_shapes=[
            pltpu.VMEM((WAVES, LEG), F32),
            pltpu.VMEM((PART * FLD, WAVES), F32),
            pltpu.VMEM((PART * FLD, WAVES), F32),
            pltpu.VMEM((LANES, LAT * FLD), F32),
        ],
        compiler_params=pltpu.CompilerParams(vmem_limit_bytes=VMEM),
        name="legendre_round",
    )(me, assignment, coeffs, to_big, from_big, depth_big, *blocks)


def mode_matrices(to_modes, from_modes, mode_depths):
    part = np.arange(PART * FLD)
    field = part // PART * FIELDS + part % FIELDS
    imag = part % PART // (HEMI * FIELDS)
    hemi = part % (HEMI * FIELDS) // FIELDS
    mode = np.arange(2 * LEVELS)
    same = (mode // LEVELS)[:, None] == imag[None, :]
    level = mode % LEVELS
    wide = to_modes[level][:, field]
    to_big = jnp.concatenate(
        [jnp.where(same & (hemi == h)[None, :], wide, 0.0) for h in range(HEMI)], axis=0
    )
    from_big = jnp.where(same.T, from_modes[field][:, level], 0.0)
    return to_big, from_big, mode_depths[level][:, None]


def body(grid, row_points, assignment, legendre, gauss_weights, to_modes, from_modes, mode_depths):
    waves = assignment.reshape(LAT, ROWS).T.reshape(1, WAVES).astype(F32)
    me = jnp.stack([lax.axis_index("fld"), lax.axis_index("lat")]).astype(jnp.int32)
    packed = pack(me, legendre, gauss_weights)
    blocks = [packed[0]] + [
        lax.ppermute(packed[t], "fld", [(i, (i + t) % FLD) for i in range(FLD)])
        for t in range(1, FLD)
    ]
    fourier = forward(row_points, waves, grid)
    coeffs = lax.all_to_all(fourier, ("fld", "lat"), 0, 0, tiled=True)
    big = mode_matrices(to_modes, from_modes, mode_depths)
    synthesis = legendre_round(me, assignment, coeffs, *big, blocks)
    back = lax.all_to_all(synthesis, ("fld", "lat"), 0, 0, tiled=True)
    return inverse(row_points, waves, back)


def solution(mesh):
    placed = (
        P(None, "lat", "fld", None),
        P("lat"),
        P(),
        P("lat", "fld", None),
        P("fld"),
        P(),
        P(),
        P(),
    )
    return jax.shard_map(
        body, mesh=mesh, in_specs=placed, out_specs=P(None, "lat", "fld", None), check_vma=False
    )
```

```python
import math

import jax
import jax.numpy as jnp
from jax import lax
from jax.experimental import pallas as pl
from jax.experimental.pallas import tpu as pltpu
from jax.sharding import PartitionSpec as P

F32 = jnp.float32
BF16 = jnp.bfloat16

HEMI = 2
ROWS = 10
FIELDS = 4
LEVELS = 32
LON = 2688
BLOCKS = LON // 128
WAVES = 640
LAT = 64
FLD = 8
PART = 2 * HEMI * FIELDS
MSG = ROWS * PART
LANES = 384
QUARTER = WAVES // 4
LEG = 896
BLOCK = FLD * ROWS
SLABS = 6
REST = SLABS * BLOCK
LMSG = REST + 24
TAIL = QUARTER - 128
WLANE = 64
FIRST = 256
VMEM = 20 << 20
UNPACK_VMEM = 58 << 20
UNPACK_COST = 10_000_000_000


def halves(x):
    top = x.astype(BF16)
    return top, (x - top.astype(F32)).astype(BF16)


def dot_split(a, b, dims):
    (ah, al), (bh, bl) = a, b
    d = (dims, ((), ()))
    out = lax.dot_general(ah, bl, d, preferred_element_type=F32)
    out = out + lax.dot_general(al, bh, d, preferred_element_type=F32)
    return out + lax.dot_general(ah, bh, d, preferred_element_type=F32)


AB = ((1,), (0,))
ABT = ((1,), (1,))


def turn(waves, points, index):
    product = waves * index
    quarter = points * 0.25
    count = jnp.floor(product * (4.0 / points) + 0.5)
    angle = (product - count * quarter) * (2.0 * math.pi / points)
    z = angle * angle
    s = angle * (
        1.0 + z * (-1 / 6 + z * (1 / 120 + z * (-1 / 5040 + z * (1 / 362880))))
    )
    c = 1.0 + z * (-0.5 + z * (1 / 24 + z * (-1 / 720 + z * (1 / 40320 - z / 3628800))))
    quad = count.astype(jnp.int32) & 3
    odd = (quad & 1) == 1
    cos_v = jnp.where(odd, s, c)
    sin_v = jnp.where(odd, c, s)
    cos_v = jnp.where((quad == 1) | (quad == 2), -cos_v, cos_v)
    sin_v = jnp.where(quad >= 2, -sin_v, sin_v)
    return cos_v, sin_v


def iota(shape, dim):
    return lax.broadcasted_iota(jnp.int32, shape, dim).astype(F32)


def tables(waves, points, cs_ref):
    c0, s0 = turn(waves, points, iota((16, WAVES), 0))
    c1, s1 = turn(waves, points, iota((8, WAVES), 0) * 16.0)
    for b in range(8):
        cb, sb = c1[b : b + 1], s1[b : b + 1]
        cs_ref[16 * b : 16 * b + 16, :WAVES] = c0 * cb - s0 * sb
        cs_ref[16 * b : 16 * b + 16, WAVES:] = s0 * cb + c0 * sb
    return turn(waves, points, iota((24, WAVES), 0) * 128.0)


def forward_kernel(points_ref, waves_ref, grid_ref, out_ref, cs_ref, fourier_ref):
    r = pl.program_id(0)
    count = points_ref[r]
    points = jnp.full((1, WAVES), count, jnp.int32).astype(F32)
    waves = waves_ref[...]
    co, so = tables(waves, points, cs_ref)
    wh, wl = halves(cs_ref[...])
    x = jnp.concatenate([grid_ref[0, 0], grid_ref[1, 0]], axis=0)
    column = lax.broadcasted_iota(jnp.int32, x.shape, 1)
    x = jnp.where(column < count, x, 0.0)
    x = jnp.concatenate([x[:, 128 * a : 128 * a + 128] for a in range(BLOCKS)], axis=0)
    xh, xl = halves(x)
    d = (AB, ((), ()))
    part = lax.dot_general(
        jnp.concatenate([xh, xl], axis=1),
        jnp.concatenate([wh, wh], axis=0),
        d,
        preferred_element_type=F32,
    ) + lax.dot_general(xh, wl, d, preferred_element_type=F32)
    re = jnp.zeros((8, WAVES), F32)
    im = jnp.zeros((8, WAVES), F32)
    for a in range(BLOCKS):
        pc = part[8 * a : 8 * a + 8, :WAVES]
        ps = part[8 * a : 8 * a + 8, WAVES:]
        ca, sa = co[a : a + 1], so[a : a + 1]
        re = re + (pc * ca - ps * sa)
        im = im - (ps * ca + pc * sa)
    scale = jnp.where(2.0 * waves < points, 1.0 / points, 0.0)
    row = pl.multiple_of(r * PART, PART)
    fourier_ref[pl.ds(row, 8), :] = re * scale
    fourier_ref[pl.ds(row + 8, 8), :] = im * scale

    @pl.when(r == ROWS - 1)
    def _():
        y = fourier_ref[...]
        shared = []
        for q in range(2):
            piece = y[:, 512 + 64 * q : 576 + 64 * q]
            shared += [jnp.concatenate([piece, piece], axis=1)] * 2
        full = jnp.concatenate(
            [
                y[:, :512],
                jnp.concatenate(shared, axis=1),
                jnp.zeros((LANES - 2 * MSG, 512), F32),
            ],
            axis=0,
        )
        out_ref[...] = full.T


def forward(row_points, waves, grid):
    return pl.pallas_call(
        forward_kernel,
        grid=(ROWS,),
        in_specs=[
            pl.BlockSpec(memory_space=pltpu.SMEM),
            pl.BlockSpec((1, WAVES), lambda r: (0, 0)),
            pl.BlockSpec((HEMI, 1, FIELDS, LON), lambda r: (0, r, 0, 0)),
        ],
        out_specs=pl.BlockSpec((LAT * FLD, LANES), lambda r: (0, 0)),
        out_shape=jax.ShapeDtypeStruct((LAT * FLD, LANES), F32),
        scratch_shapes=[
            pltpu.VMEM((128, 2 * WAVES), F32),
            pltpu.VMEM((MSG, WAVES), F32),
        ],
        compiler_params=pltpu.CompilerParams(vmem_limit_bytes=VMEM),
        cost_estimate=pl.CostEstimate(
            flops=3_000_000_000, bytes_accessed=2_000_000, transcendentals=0
        ),
        name="forward_fourier",
    )(row_points, waves, grid)


def inverse_kernel(points_ref, waves_ref, coeff_ref, out_ref, cs_ref, fourier_ref):
    r = pl.program_id(0)

    @pl.when(r == 0)
    def _():
        t = coeff_ref[...].T
        fourier_ref[:, :512] = t[:MSG]
        lane = lax.broadcasted_iota(jnp.int32, (MSG, 128), 1)
        sums = []
        for q in range(2):
            s = t[MSG : 2 * MSG, 256 * q : 256 * q + 128]
            s = s + t[MSG : 2 * MSG, 256 * q + 128 : 256 * q + 256]
            sums.append(s + pltpu.roll(s, 64, 1))
        fourier_ref[:, 512:] = jnp.where(lane < 64, sums[0], sums[1])

    count = points_ref[r]
    points = jnp.full((1, WAVES), count, jnp.int32).astype(F32)
    waves = waves_ref[...]
    co, so = tables(waves, points, cs_ref)
    wh, wl = halves(cs_ref[...])
    weight = jnp.where(2.0 * waves < points, jnp.where(waves == 0.0, 1.0, 2.0), 0.0)
    row = pl.multiple_of(r * PART, PART)
    re = fourier_ref[pl.ds(row, 8), :] * weight
    im = fourier_ref[pl.ds(row + 8, 8), :] * weight
    cosine, sine = [], []
    for a in range(BLOCKS):
        ca, sa = co[a : a + 1], so[a : a + 1]
        cosine.append(re * ca - im * sa)
        sine.append(-(re * sa + im * ca))
    turned = jnp.concatenate(
        [jnp.concatenate(cosine, axis=0), jnp.concatenate(sine, axis=0)], axis=1
    )
    th, tl = halves(turned)
    d = (ABT, ((), ()))
    both = lax.dot_general(
        th, jnp.concatenate([wh, wl], axis=0), d, preferred_element_type=F32
    )
    values = both[:, :128] + both[:, 128:]
    values = values + lax.dot_general(tl, wh, d, preferred_element_type=F32)
    wide = jnp.concatenate(
        [values[8 * a : 8 * a + 8] for a in range(BLOCKS)], axis=1
    )
    column = lax.broadcasted_iota(jnp.int32, wide.shape, 1)
    wide = jnp.where(column < count, wide, 0.0)
    out_ref[0, 0] = wide[:FIELDS]
    out_ref[1, 0] = wide[FIELDS:]


def inverse(row_points, waves, coeffs):
    return pl.pallas_call(
        inverse_kernel,
        grid=(ROWS,),
        in_specs=[
            pl.BlockSpec(memory_space=pltpu.SMEM),
            pl.BlockSpec((1, WAVES), lambda r: (0, 0)),
            pl.BlockSpec((LAT * FLD, LANES), lambda r: (0, 0)),
        ],
        out_specs=pl.BlockSpec((HEMI, 1, FIELDS, LON), lambda r: (0, r, 0, 0)),
        out_shape=jax.ShapeDtypeStruct((HEMI, ROWS, FIELDS, LON), F32),
        scratch_shapes=[
            pltpu.VMEM((128, 2 * WAVES), F32),
            pltpu.VMEM((MSG, WAVES), F32),
        ],
        compiler_params=pltpu.CompilerParams(vmem_limit_bytes=VMEM),
        name="inverse_fourier",
    )(row_points, waves, coeffs)


def pack_kernel(me_ref, legendre_ref, weight_ref, *refs):
    near_refs = {0: refs[0], 1: refs[1], 7: refs[2]}
    up_ref, down_ref, tile_ref = refs[3:]
    me = me_ref[0]
    lane = lax.broadcasted_iota(jnp.int32, (BLOCK, 128), 1)
    weight = jnp.concatenate(
        [weight_ref[...], jnp.zeros((FLD, 128 - ROWS), F32)], axis=1
    )
    weight = pltpu.roll(weight, WLANE, 1)
    for t in range(FLD):

        def store(row, value, t=t):
            if t in (0, 1, 7):
                ref, at = near_refs[t], row
            elif t < 4:
                ref, at = up_ref, (t - 2) * LMSG + row
            elif t > 4:
                ref, at = down_ref, (6 - t) * LMSG + row
            elif row < FIRST:
                ref, at = up_ref, 2 * LMSG + row
            else:
                ref, at = down_ref, 2 * LMSG + row - FIRST
            ref[pl.ds(at, FLD), :] = value

        g = lax.rem(me + t, FLD)
        shared = FLD + g // 4
        shift = lax.rem(WAVES - QUARTER * lax.rem(g, 4), WAVES)
        quarter = pltpu.roll(legendre_ref[shared], shift, 1)
        own = legendre_ref[g]
        for i in range(5):
            tile_ref[t, i] = own[:, 128 * i : 128 * i + 128]
        tile_ref[t, 5] = quarter[:, :128]
        tile_ref[t, 6] = jnp.where(lane < TAIL, quarter[:, 128:256], 0.0)
        for i in range(SLABS):
            for r in range(ROWS):
                rows = pl.ds(r, FLD, stride=ROWS)
                store(BLOCK * i + FLD * r, tile_ref[t, i, rows, :])
        for i in range(3):
            rest = weight if i == 2 else jnp.zeros((FLD, 128), F32)
            for r in range(4 * i, min(4 * i + 4, ROWS)):
                part = tile_ref[t, 6, pl.ds(r, FLD, stride=ROWS), :]
                rest = rest + (pltpu.roll(part, TAIL * (r % 4), 1) if r % 4 else part)
            store(REST + FLD * i, rest)


def pack(me, legendre, gauss_weights):
    vmem = pl.BlockSpec(memory_space=pltpu.VMEM)
    rows = (LMSG, LMSG, LMSG, 2 * LMSG + FIRST, 3 * LMSG - FIRST)
    return pl.pallas_call(
        pack_kernel,
        in_specs=[pl.BlockSpec(memory_space=pltpu.SMEM), vmem, vmem],
        out_specs=[vmem] * 5,
        out_shape=[jax.ShapeDtypeStruct((n, 128), F32) for n in rows],
        scratch_shapes=[pltpu.VMEM((FLD, LEG // 128, BLOCK, 128), F32)],
        compiler_params=pltpu.CompilerParams(vmem_limit_bytes=VMEM),
        name="pack_legendre",
    )(me, legendre, gauss_weights.reshape(FLD, ROWS))


def shift(x, step):
    return lax.ppermute(x, "fld", [(i, (i + step) % FLD) for i in range(FLD)])


def ring(up1, down1, up2, down2):
    up2, down2 = shift(up2, 2), shift(down2, -2)
    up1, down1 = shift(up1, 1), shift(down1, -1)
    up3, down3 = shift(up2[LMSG : 2 * LMSG], 1), shift(down2[LMSG : 2 * LMSG], -1)
    up4, down4 = shift(up2[2 * LMSG :], 2), shift(down2[2 * LMSG :], -2)
    return up1, up2, up3, up4, down1, down2, down3, down4


def mode_matrices(to_modes, from_modes):
    def ids(shape, dim):
        return lax.broadcasted_iota(jnp.int32, shape, dim)

    def product(a, b):
        return lax.dot_general(
            a, b, (AB, ((), ())), precision=lax.Precision.HIGHEST, preferred_element_type=F32
        )

    def field(part):
        return part // PART * FIELDS + part % FIELDS

    parts, modes = PART * FLD, 2 * LEVELS
    spread = (ids((LEVELS, parts), 0) == field(ids((LEVELS, parts), 1))).astype(F32)
    double = (ids((parts, LEVELS), 0) % LEVELS == ids((parts, LEVELS), 1)).astype(F32)
    wide = product(double, product(to_modes, spread))
    row, part = ids((parts, parts), 0), ids((parts, parts), 1) % PART
    to_big = jnp.where(
        (row // LEVELS % 2 == part // 8) & (row // modes == part % 8 // FIELDS), wide, 0.0
    )
    spread = (field(ids((parts, LEVELS), 0)) == ids((parts, LEVELS), 1)).astype(F32)
    double = (ids((LEVELS, modes), 0) == ids((LEVELS, modes), 1) % LEVELS).astype(F32)
    wide = product(product(spread, from_modes), double)
    part, column = ids((parts, modes), 0) % PART, ids((parts, modes), 1)
    return to_big, jnp.where(part // 8 == column // LEVELS, wide, 0.0)


def unpack_kernel(me_ref, own_msg, *refs):
    ups, downs, (leg_ref, weight_ref) = refs[:4], refs[4:8], refs[8:]
    fld = me_ref[0]
    lane = lax.broadcasted_iota(jnp.int32, (FLD, 128), 1)
    for t in range(FLD):

        def load(row, t=t):
            if t == 0:
                return own_msg[row : row + FLD]
            if t < 4:
                return ups[t - 1][row : row + FLD]
            if t > 4:
                return downs[7 - t][row : row + FLD]
            if row < FIRST:
                return ups[3][row : row + FLD]
            return downs[3][row - FIRST : row - FIRST + FLD]

        source = lax.rem(fld + FLD - t, FLD)
        for r in range(ROWS):
            place = pl.ds(pl.multiple_of(r * LAT + FLD * source, FLD), FLD)
            for i in range(SLABS):
                leg_ref[place, 128 * i : 128 * i + 128] = load(BLOCK * i + FLD * r)
            rest = load(REST + FLD * (r // 4))
            if r % 4:
                rest = pltpu.roll(rest, 128 - TAIL * (r % 4), 1)
            leg_ref[place, 768:] = jnp.where(lane < TAIL, rest, 0.0)
        weight_ref[pl.ds(pl.multiple_of(FLD * source, FLD), FLD), :] = load(REST + 2 * FLD)


def unpack(me, own, moved):
    vmem = pl.BlockSpec(memory_space=pltpu.VMEM)
    taken = [
        pl.BlockSpec((min(LMSG, x.shape[0]), 128), lambda i: (0, 0)) for x in moved
    ]
    return pl.pallas_call(
        unpack_kernel,
        grid=(1,),
        in_specs=[pl.BlockSpec(memory_space=pltpu.SMEM), vmem] + taken,
        out_specs=[vmem, vmem],
        out_shape=[
            jax.ShapeDtypeStruct((WAVES, LEG), F32),
            jax.ShapeDtypeStruct((LAT, 128), F32),
        ],
        compiler_params=pltpu.CompilerParams(vmem_limit_bytes=UNPACK_VMEM),
        cost_estimate=pl.CostEstimate(
            flops=UNPACK_COST, bytes_accessed=5_000_000, transcendentals=0
        ),
        name="unpack_legendre",
    )(me, own, *moved)


def legendre_kernel(
    me_ref,
    assignment_ref,
    coeff_ref,
    to_ref,
    from_ref,
    depth_ref,
    leg_ref,
    weight_ref,
    out_ref,
    a_ref,
    x_ref,
    y_ref,
):
    lat, fld = me_ref[1], me_ref[0]
    weight = weight_ref[...].T
    weight = jnp.concatenate(
        [weight[WLANE + r : WLANE + r + 1] for r in range(ROWS)], axis=1
    )
    lh, ll = halves(leg_ref[...])

    t = coeff_ref[...].T
    for kind, dest in ((0, a_ref), (1, x_ref)):
        for u in range(ROWS // 2):
            row = kind * MSG + 2 * u * PART
            even, odd = t[row : row + PART], t[row + PART : row + 2 * PART]
            for g in range(FLD):
                cut = slice(LAT * g, LAT * g + LAT)
                dest[PART * g : PART * g + PART, 128 * u : 128 * u + 128] = (
                    jnp.concatenate([even[:, cut], odd[:, cut]], axis=1)
                )
    own = halves(a_ref[...] * weight)
    shared = halves(x_ref[...] * weight)
    spectrum = jnp.concatenate(
        [
            dot_split(own, (lh[:, :WAVES], ll[:, :WAVES]), AB),
            dot_split(shared, (lh[:, WAVES:], ll[:, WAVES:]), AB),
        ],
        axis=1,
    )

    to_big, from_big = mode_matrices(to_ref[...], from_ref[...])
    modes = dot_split(halves(to_big), halves(spectrum), AB)
    lane = lax.broadcasted_iota(jnp.int32, (1, LEG), 1)
    is_own = lane < WAVES
    degree = jnp.where(is_own, lane, lane - WAVES + QUARTER * lax.rem(fld, 4))
    wave_own = assignment_ref[lat * ROWS + fld]
    wave_shared = assignment_ref[lat * ROWS + FLD + fld // 4]
    total = degree + jnp.where(is_own, wave_own, wave_shared)
    within = (total < WAVES) & (lane < WAVES + QUARTER)
    total = jnp.where(within, total, 0)
    sign = jnp.where((degree & 1) == 0, 1.0, -1.0)
    ratio = (total * (total + 1)).astype(F32) * (1.0 / (WAVES * (WAVES + 1)))
    half = 2 * LEVELS
    depth = jnp.concatenate([depth_ref[...], depth_ref[...]], axis=0)
    modes = modes[:half] + sign * modes[half:]
    modes = jnp.where(within, modes, 0.0) / (1.0 + depth * ratio)
    updated = dot_split(halves(from_big), halves(modes), AB)
    row_id = lax.broadcasted_iota(jnp.int32, updated.shape, 0)
    updated = jnp.where((row_id & FIELDS) == 0, updated, updated * sign)

    for kind, cols in ((0, slice(0, WAVES)), (1, slice(WAVES, LEG))):
        back = dot_split(halves(updated[:, cols]), (lh[:, cols], ll[:, cols]), ABT)
        for u in range(ROWS // 2):
            row = kind * MSG + 2 * u * PART
            for g in range(0, FLD, 2):
                one = back[PART * g : PART * g + PART, 128 * u : 128 * u + 128]
                two = back[PART * g + PART : PART * g + 2 * PART, 128 * u : 128 * u + 128]
                for odd in range(2):
                    cut = slice(64 * odd, 64 * odd + 64)
                    y_ref[
                        row + PART * odd : row + PART * odd + PART, LAT * g : LAT * g + 128
                    ] = jnp.concatenate([one[:, cut], two[:, cut]], axis=1)
    y_ref[2 * MSG :, :] = jnp.zeros((LANES - 2 * MSG, LAT * FLD), F32)
    out_ref[...] = y_ref[...].T


def legendre_round(*args):
    smem = pl.BlockSpec(memory_space=pltpu.SMEM)
    vmem = pl.BlockSpec(memory_space=pltpu.VMEM)
    return pl.pallas_call(
        legendre_kernel,
        in_specs=[smem, smem] + [vmem] * 6,
        out_specs=vmem,
        out_shape=jax.ShapeDtypeStruct((LAT * FLD, LANES), F32),
        scratch_shapes=[
            pltpu.VMEM((PART * FLD, WAVES), F32),
            pltpu.VMEM((PART * FLD, WAVES), F32),
            pltpu.VMEM((LANES, LAT * FLD), F32),
        ],
        compiler_params=pltpu.CompilerParams(vmem_limit_bytes=VMEM),
        name="legendre_round",
    )(*args)


def body(grid, row_points, assignment, legendre, gauss_weights, to_modes, from_modes, mode_depths):
    waves = assignment.reshape(LAT, ROWS).T.reshape(1, WAVES).astype(F32)
    me = jnp.stack([lax.axis_index("fld"), lax.axis_index("lat")]).astype(jnp.int32)
    own, *messages = pack(me, legendre, gauss_weights)
    waves, own = lax.optimization_barrier((waves, own))
    rows, weight = unpack(me, own, ring(*messages))
    fourier = forward(row_points, waves, grid)
    coeffs = lax.all_to_all(fourier, ("fld", "lat"), 0, 0, tiled=True)
    depths = mode_depths.reshape(LEVELS, 1)
    synthesis = legendre_round(
        me, assignment, coeffs, to_modes, from_modes, depths, rows, weight
    )
    back = lax.all_to_all(synthesis, ("fld", "lat"), 0, 0, tiled=True)
    return inverse(row_points, waves, back)


def solution(mesh):
    placed = (
        P(None, "lat", "fld", None),
        P("lat"),
        P(),
        P("lat", "fld", None),
        P("fld"),
        P(),
        P(),
        P(),
    )
    return jax.shard_map(
        body, mesh=mesh, in_specs=placed, out_specs=P(None, "lat", "fld", None), check_vma=False
    )
```

```python
import math

import jax
import jax.numpy as jnp
from jax import lax
from jax.experimental import pallas as pl
from jax.experimental.pallas import tpu as pltpu
from jax.sharding import PartitionSpec as P

F32 = jnp.float32
BF16 = jnp.bfloat16

HEMI = 2
ROWS = 10
FIELDS = 4
LEVELS = 32
LON = 2688
BLOCKS = LON // 128
WAVES = 640
LAT = 64
FLD = 8
PART = 2 * HEMI * FIELDS
MSG = ROWS * PART
HALF_MSG = MSG // 2
LANES = 256
QUARTER = WAVES // 4
LEG = 896
BLOCK = FLD * ROWS
SLABS = 6
REST = SLABS * BLOCK
LMSG = REST + 24
TAIL = QUARTER - 128
WLANE = 64
FIRST = 256
VMEM = 20 << 20
UNPACK_VMEM = 50 << 20
UNPACK_COST = 9_000_000_000


def halves(x):
    top = x.astype(BF16)
    return top, (x - top.astype(F32)).astype(BF16)


def dot_split(a, b, dims):
    (ah, al), (bh, bl) = a, b
    d = (dims, ((), ()))
    out = lax.dot_general(ah, bl, d, preferred_element_type=F32)
    out = out + lax.dot_general(al, bh, d, preferred_element_type=F32)
    return out + lax.dot_general(ah, bh, d, preferred_element_type=F32)


AB = ((1,), (0,))
ABT = ((1,), (1,))


def turn(waves, points, index):
    product = waves * index
    quarter = points * 0.25
    count = jnp.floor(product * (4.0 / points) + 0.5)
    angle = (product - count * quarter) * (2.0 * math.pi / points)
    z = angle * angle
    s = angle * (
        1.0 + z * (-1 / 6 + z * (1 / 120 + z * (-1 / 5040 + z * (1 / 362880))))
    )
    c = 1.0 + z * (-0.5 + z * (1 / 24 + z * (-1 / 720 + z * (1 / 40320 - z / 3628800))))
    quad = count.astype(jnp.int32) & 3
    odd = (quad & 1) == 1
    cos_v = jnp.where(odd, s, c)
    sin_v = jnp.where(odd, c, s)
    cos_v = jnp.where((quad == 1) | (quad == 2), -cos_v, cos_v)
    sin_v = jnp.where(quad >= 2, -sin_v, sin_v)
    return cos_v, sin_v


def iota(shape, dim):
    return lax.broadcasted_iota(jnp.int32, shape, dim).astype(F32)


def tables(waves, points, cs_ref):
    c0, s0 = turn(waves, points, iota((16, WAVES), 0))
    c1, s1 = turn(waves, points, iota((8, WAVES), 0) * 16.0)
    for b in range(8):
        cb, sb = c1[b : b + 1], s1[b : b + 1]
        cs_ref[16 * b : 16 * b + 16, :WAVES] = c0 * cb - s0 * sb
        cs_ref[16 * b : 16 * b + 16, WAVES:] = s0 * cb + c0 * sb
    return turn(waves, points, iota((24, WAVES), 0) * 128.0)


def forward_kernel(points_ref, waves_ref, grid_ref, out_ref, cs_ref, fourier_ref):
    r = pl.program_id(0)
    count = points_ref[r]
    points = jnp.full((1, WAVES), count, jnp.int32).astype(F32)
    waves = waves_ref[...]
    co, so = tables(waves, points, cs_ref)
    wh, wl = halves(cs_ref[...])
    x = jnp.concatenate([grid_ref[0, 0], grid_ref[1, 0]], axis=0)
    column = lax.broadcasted_iota(jnp.int32, x.shape, 1)
    x = jnp.where(column < count, x, 0.0)
    x = jnp.concatenate([x[:, 128 * a : 128 * a + 128] for a in range(BLOCKS)], axis=0)
    xh, xl = halves(x)
    d = (AB, ((), ()))
    part = lax.dot_general(
        jnp.concatenate([xh, xl], axis=1),
        jnp.concatenate([wh, wh], axis=0),
        d,
        preferred_element_type=F32,
    ) + lax.dot_general(xh, wl, d, preferred_element_type=F32)
    re = jnp.zeros((8, WAVES), F32)
    im = jnp.zeros((8, WAVES), F32)
    for a in range(BLOCKS):
        pc = part[8 * a : 8 * a + 8, :WAVES]
        ps = part[8 * a : 8 * a + 8, WAVES:]
        ca, sa = co[a : a + 1], so[a : a + 1]
        re = re + (pc * ca - ps * sa)
        im = im - (ps * ca + pc * sa)
    scale = jnp.where(2.0 * waves < points, 1.0 / points, 0.0)
    row = pl.multiple_of(r * PART, PART)
    fourier_ref[pl.ds(row, 8), :] = re * scale
    fourier_ref[pl.ds(row + 8, 8), :] = im * scale

    @pl.when(r == ROWS - 1)
    def _():
        y = fourier_ref[...]
        top = lax.broadcasted_iota(jnp.int32, (8, 128), 0) < FIELDS
        low = lax.broadcasted_iota(jnp.int32, (8, 128), 1) < 64
        shared = []
        for row in range(0, MSG, PART):
            re, im = y[row : row + 8, 512:], y[row + 8 : row + PART, 512:]
            re_other, im_other = pltpu.roll(re, FIELDS, 0), pltpu.roll(im, FIELDS, 0)
            total = jnp.where(top, re + re_other, im + im_other)
            change = jnp.where(top, re - re_other, im_other - im)
            first = jnp.where(low, total, pltpu.roll(change, 64, 1))
            second = jnp.where(low, pltpu.roll(total, 64, 1), change)
            shared.append(jnp.concatenate([first, first, second, second], axis=1))
        pad = jnp.zeros((LANES - MSG - HALF_MSG, 512), F32)
        full = jnp.concatenate([y[:, :512], *shared, pad], axis=0)
        out_ref[...] = full.T


def forward(row_points, waves, grid):
    return pl.pallas_call(
        forward_kernel,
        grid=(ROWS,),
        in_specs=[
            pl.BlockSpec(memory_space=pltpu.SMEM),
            pl.BlockSpec((1, WAVES), lambda r: (0, 0)),
            pl.BlockSpec((HEMI, 1, FIELDS, LON), lambda r: (0, r, 0, 0)),
        ],
        out_specs=pl.BlockSpec((LAT * FLD, LANES), lambda r: (0, 0)),
        out_shape=jax.ShapeDtypeStruct((LAT * FLD, LANES), F32),
        scratch_shapes=[
            pltpu.VMEM((128, 2 * WAVES), F32),
            pltpu.VMEM((MSG, WAVES), F32),
        ],
        compiler_params=pltpu.CompilerParams(vmem_limit_bytes=VMEM),
        cost_estimate=pl.CostEstimate(
            flops=3_000_000_000, bytes_accessed=2_000_000, transcendentals=0
        ),
        name="forward_fourier",
    )(row_points, waves, grid)


def inverse_kernel(points_ref, waves_ref, coeff_ref, out_ref, cs_ref, fourier_ref):
    r = pl.program_id(0)

    @pl.when(r == 0)
    def _():
        t = coeff_ref[...].T
        fourier_ref[:, :512] = t[:MSG]
        top = lax.broadcasted_iota(jnp.int32, (8, 128), 0) < FIELDS
        low = lax.broadcasted_iota(jnp.int32, (8, 128), 1) < 64
        for i in range(ROWS):
            rows = slice(MSG + 8 * i, MSG + 8 * i + 8)
            one = t[rows, :128] + t[rows, 128:256]
            two = t[rows, 256:384] + t[rows, 384:]
            one_other, two_other = pltpu.roll(one, 64, 1), pltpu.roll(two, 64, 1)
            north = jnp.where(low, one + one_other, two + two_other)
            south = jnp.where(low, one - one_other, two_other - two)
            fourier_ref[PART * i : PART * i + 8, 512:] = jnp.where(
                top, north, pltpu.roll(south, FIELDS, 0)
            )
            fourier_ref[PART * i + 8 : PART * i + PART, 512:] = jnp.where(
                top, pltpu.roll(north, FIELDS, 0), south
            )

    count = points_ref[r]
    points = jnp.full((1, WAVES), count, jnp.int32).astype(F32)
    waves = waves_ref[...]
    co, so = tables(waves, points, cs_ref)
    wh, wl = halves(cs_ref[...])
    weight = jnp.where(2.0 * waves < points, jnp.where(waves == 0.0, 1.0, 2.0), 0.0)
    row = pl.multiple_of(r * PART, PART)
    re = fourier_ref[pl.ds(row, 8), :] * weight
    im = fourier_ref[pl.ds(row + 8, 8), :] * weight
    cosine, sine = [], []
    for a in range(BLOCKS):
        ca, sa = co[a : a + 1], so[a : a + 1]
        cosine.append(re * ca - im * sa)
        sine.append(-(re * sa + im * ca))
    turned = jnp.concatenate(
        [jnp.concatenate(cosine, axis=0), jnp.concatenate(sine, axis=0)], axis=1
    )
    th, tl = halves(turned)
    d = (ABT, ((), ()))
    both = lax.dot_general(
        th, jnp.concatenate([wh, wl], axis=0), d, preferred_element_type=F32
    )
    values = both[:, :128] + both[:, 128:]
    values = values + lax.dot_general(tl, wh, d, preferred_element_type=F32)
    wide = jnp.concatenate(
        [values[8 * a : 8 * a + 8] for a in range(BLOCKS)], axis=1
    )
    column = lax.broadcasted_iota(jnp.int32, wide.shape, 1)
    wide = jnp.where(column < count, wide, 0.0)
    out_ref[0, 0] = wide[:FIELDS]
    out_ref[1, 0] = wide[FIELDS:]


def inverse(row_points, waves, coeffs):
    return pl.pallas_call(
        inverse_kernel,
        grid=(ROWS,),
        in_specs=[
            pl.BlockSpec(memory_space=pltpu.SMEM),
            pl.BlockSpec((1, WAVES), lambda r: (0, 0)),
            pl.BlockSpec((LAT * FLD, LANES), lambda r: (0, 0)),
        ],
        out_specs=pl.BlockSpec((HEMI, 1, FIELDS, LON), lambda r: (0, r, 0, 0)),
        out_shape=jax.ShapeDtypeStruct((HEMI, ROWS, FIELDS, LON), F32),
        scratch_shapes=[
            pltpu.VMEM((128, 2 * WAVES), F32),
            pltpu.VMEM((MSG, WAVES), F32),
        ],
        compiler_params=pltpu.CompilerParams(vmem_limit_bytes=VMEM),
        name="inverse_fourier",
    )(row_points, waves, coeffs)


def quarter_degree(place):
    quarter = sum((place >= QUARTER * i).astype(jnp.int32) for i in range(1, 4))
    inside = place - QUARTER * quarter
    return 2 * (QUARTER * (quarter >> 1) + inside) + (quarter & 1)


def permuted(x, one_hot):
    out = None
    parts = []
    for _ in range(3):
        parts.append(x.astype(BF16))
        x = x - parts[-1].astype(F32)
    for part in reversed(parts):
        moved = lax.dot_general(part, one_hot, (AB, ((), ())), preferred_element_type=F32)
        out = moved if out is None else out + moved
    return out


def pack_kernel(me_ref, legendre_ref, weight_ref, *refs):
    near_refs = {0: refs[0], 1: refs[1], 7: refs[2]}
    up_ref, down_ref, tile_ref, order_ref = refs[3:]
    me = me_ref[0]
    lane = lax.broadcasted_iota(jnp.int32, (BLOCK, 128), 1)
    weight = jnp.concatenate(
        [weight_ref[...], jnp.zeros((FLD, 128 - ROWS), F32)], axis=1
    )
    weight = pltpu.roll(weight, WLANE, 1)
    place = lax.broadcasted_iota(jnp.int32, (WAVES, WAVES), 1)
    degree = lax.broadcasted_iota(jnp.int32, (WAVES, WAVES), 0)
    one_hot = (degree == quarter_degree(place)).astype(BF16)
    for q in range(2):
        order_ref[q] = permuted(legendre_ref[FLD + q], one_hot)
    for t in range(FLD):

        def store(row, value, t=t):
            if t in (0, 1, 7):
                ref, at = near_refs[t], row
            elif t < 4:
                ref, at = up_ref, (t - 2) * LMSG + row
            elif t > 4:
                ref, at = down_ref, (6 - t) * LMSG + row
            elif row < FIRST:
                ref, at = up_ref, 2 * LMSG + row
            else:
                ref, at = down_ref, 2 * LMSG + row - FIRST
            ref[pl.ds(at, FLD), :] = value

        g = lax.rem(me + t, FLD)
        shift = lax.rem(WAVES - QUARTER * lax.rem(g, 4), WAVES)
        quarter = pltpu.roll(order_ref[g // 4], shift, 1)
        own = legendre_ref[g]
        for i in range(5):
            tile_ref[t, i] = own[:, 128 * i : 128 * i + 128]
        tile_ref[t, 5] = quarter[:, :128]
        tile_ref[t, 6] = jnp.where(lane < TAIL, quarter[:, 128:256], 0.0)
        for i in range(SLABS):
            for r in range(ROWS):
                rows = pl.ds(r, FLD, stride=ROWS)
                store(BLOCK * i + FLD * r, tile_ref[t, i, rows, :])
        for i in range(3):
            rest = weight if i == 2 else jnp.zeros((FLD, 128), F32)
            for r in range(4 * i, min(4 * i + 4, ROWS)):
                part = tile_ref[t, 6, pl.ds(r, FLD, stride=ROWS), :]
                rest = rest + (pltpu.roll(part, TAIL * (r % 4), 1) if r % 4 else part)
            store(REST + FLD * i, rest)


def pack(me, legendre, gauss_weights):
    vmem = pl.BlockSpec(memory_space=pltpu.VMEM)
    rows = (LMSG, LMSG, LMSG, 2 * LMSG + FIRST, 3 * LMSG - FIRST)
    return pl.pallas_call(
        pack_kernel,
        in_specs=[pl.BlockSpec(memory_space=pltpu.SMEM), vmem, vmem],
        out_specs=[vmem] * 5,
        out_shape=[jax.ShapeDtypeStruct((n, 128), F32) for n in rows],
        scratch_shapes=[
            pltpu.VMEM((FLD, LEG // 128, BLOCK, 128), F32),
            pltpu.VMEM((2, BLOCK, WAVES), F32),
        ],
        compiler_params=pltpu.CompilerParams(vmem_limit_bytes=VMEM),
        name="pack_legendre",
    )(me, legendre, gauss_weights.reshape(FLD, ROWS))


def shift(x, step):
    return lax.ppermute(x, "fld", [(i, (i + step) % FLD) for i in range(FLD)])


def ring(up1, down1, up2, down2):
    up2, down2 = shift(up2, 2), shift(down2, -2)
    up1, down1 = shift(up1, 1), shift(down1, -1)
    up3, down3 = shift(up2[LMSG : 2 * LMSG], 1), shift(down2[LMSG : 2 * LMSG], -1)
    up4, down4 = shift(up2[2 * LMSG :], 2), shift(down2[2 * LMSG :], -2)
    return up1, up2, up3, up4, down1, down2, down3, down4


def mode_matrices(to_modes, from_modes):
    def ids(shape, dim):
        return lax.broadcasted_iota(jnp.int32, shape, dim)

    def product(a, b):
        return lax.dot_general(
            a, b, (AB, ((), ())), precision=lax.Precision.HIGHEST, preferred_element_type=F32
        )

    def field(part):
        return part // PART * FIELDS + part % FIELDS

    parts, modes = PART * FLD, 2 * LEVELS
    spread = (ids((LEVELS, parts), 0) == field(ids((LEVELS, parts), 1))).astype(F32)
    double = (ids((parts, LEVELS), 0) % LEVELS == ids((parts, LEVELS), 1)).astype(F32)
    wide = product(double, product(to_modes, spread))
    row, part = ids((parts, parts), 0), ids((parts, parts), 1) % PART
    to_big = jnp.where(
        (row // LEVELS % 2 == part // 8) & (row // modes == part % 8 // FIELDS), wide, 0.0
    )
    spread = (field(ids((parts, LEVELS), 0)) == ids((parts, LEVELS), 1)).astype(F32)
    double = (ids((LEVELS, modes), 0) == ids((LEVELS, modes), 1) % LEVELS).astype(F32)
    wide = product(product(spread, from_modes), double)
    part, column = ids((parts, modes), 0) % PART, ids((parts, modes), 1)
    from_big = jnp.where(part // 8 == column // LEVELS, wide, 0.0)

    def half_field(part):
        return part // 8 * FIELDS + part % FIELDS

    spread = (ids((LEVELS, modes), 0) == half_field(ids((LEVELS, modes), 1))).astype(F32)
    double = (ids((modes, LEVELS), 0) % LEVELS == ids((modes, LEVELS), 1)).astype(F32)
    wide = product(double, product(to_modes, spread))
    row, column = ids((modes, modes), 0), ids((modes, modes), 1)
    to_half = jnp.where(row // LEVELS == column % 8 // FIELDS, wide, 0.0)
    spread = (half_field(ids((modes, LEVELS), 0)) == ids((modes, LEVELS), 1)).astype(F32)
    double = (ids((LEVELS, modes), 0) == ids((LEVELS, modes), 1) % LEVELS).astype(F32)
    wide = product(product(spread, from_modes), double)
    from_half = jnp.where(row % 8 // FIELDS == column // LEVELS, wide, 0.0)
    return to_big, from_big, to_half, from_half


def unpack_kernel(me_ref, own_msg, *refs):
    ups, downs, (leg_ref, weight_ref) = refs[:4], refs[4:8], refs[8:]
    fld = me_ref[0]
    lane = lax.broadcasted_iota(jnp.int32, (FLD, 128), 1)
    for t in range(FLD):

        def load(row, t=t):
            if t == 0:
                return own_msg[row : row + FLD]
            if t < 4:
                return ups[t - 1][row : row + FLD]
            if t > 4:
                return downs[7 - t][row : row + FLD]
            if row < FIRST:
                return ups[3][row : row + FLD]
            return downs[3][row - FIRST : row - FIRST + FLD]

        source = lax.rem(fld + FLD - t, FLD)
        for r in range(ROWS):
            place = pl.ds(pl.multiple_of(r * LAT + FLD * source, FLD), FLD)
            for i in range(SLABS):
                leg_ref[place, 128 * i : 128 * i + 128] = load(BLOCK * i + FLD * r)
            rest = load(REST + FLD * (r // 4))
            if r % 4:
                rest = pltpu.roll(rest, 128 - TAIL * (r % 4), 1)
            leg_ref[place, 768:] = jnp.where(lane < TAIL, rest, 0.0)
        weight_ref[pl.ds(pl.multiple_of(FLD * source, FLD), FLD), :] = load(REST + 2 * FLD)


def unpack(me, own, moved):
    vmem = pl.BlockSpec(memory_space=pltpu.VMEM)
    taken = [
        pl.BlockSpec((min(LMSG, x.shape[0]), 128), lambda i: (0, 0)) for x in moved
    ]
    return pl.pallas_call(
        unpack_kernel,
        grid=(1,),
        in_specs=[pl.BlockSpec(memory_space=pltpu.SMEM), vmem] + taken,
        out_specs=[vmem, vmem],
        out_shape=[
            jax.ShapeDtypeStruct((WAVES, LEG), F32),
            jax.ShapeDtypeStruct((LAT, 128), F32),
        ],
        compiler_params=pltpu.CompilerParams(vmem_limit_bytes=UNPACK_VMEM),
        cost_estimate=pl.CostEstimate(
            flops=UNPACK_COST, bytes_accessed=5_000_000, transcendentals=0
        ),
        name="unpack_legendre",
    )(me, own, *moved)


def legendre_kernel(
    me_ref,
    assignment_ref,
    coeff_ref,
    to_ref,
    from_ref,
    depth_ref,
    leg_ref,
    weight_ref,
    out_ref,
    a_ref,
    x_ref,
    y_ref,
):
    lat, fld = me_ref[1], me_ref[0]
    weight = weight_ref[...].T
    weight = jnp.concatenate(
        [weight[WLANE + r : WLANE + r + 1] for r in range(ROWS)], axis=1
    )
    lh, ll = halves(leg_ref[...])

    t = coeff_ref[...].T
    for start, part, dest in ((0, PART, a_ref), (MSG, 8, x_ref)):
        for u in range(ROWS // 2):
            row = start + 2 * u * part
            even, odd = t[row : row + part], t[row + part : row + 2 * part]
            for g in range(FLD):
                cut = slice(LAT * g, LAT * g + LAT)
                dest[part * g : part * g + part, 128 * u : 128 * u + 128] = (
                    jnp.concatenate([even[:, cut], odd[:, cut]], axis=1)
                )
    own = halves(a_ref[...] * weight)
    shared = halves(x_ref[...] * weight)
    to_big, from_big, to_half, from_half = mode_matrices(to_ref[...], from_ref[...])
    spectrum = dot_split(own, (lh[:, :WAVES], ll[:, :WAVES]), AB)
    modes = dot_split(halves(to_big), halves(spectrum), AB)
    spectrum = dot_split(shared, (lh[:, WAVES:], ll[:, WAVES:]), AB)
    modes_shared = dot_split(halves(to_half), halves(spectrum), AB)

    lane = lax.broadcasted_iota(jnp.int32, (1, LEG), 1)
    is_own = lane < WAVES
    quarter = lax.rem(fld, 4)
    place = QUARTER * (quarter // 2) + lane - WAVES
    degree = jnp.where(is_own, lane, 2 * place + lax.rem(quarter, 2))
    wave_own = assignment_ref[lat * ROWS + fld]
    wave_shared = assignment_ref[lat * ROWS + FLD + fld // 4]
    total = degree + jnp.where(is_own, wave_own, wave_shared)
    within = (total < WAVES) & (lane < WAVES + QUARTER)
    total = jnp.where(within, total, 0)
    sign = jnp.where((degree & 1) == 0, 1.0, -1.0)[:, :WAVES]
    ratio = (total * (total + 1)).astype(F32) * (1.0 / (WAVES * (WAVES + 1)))
    half = 2 * LEVELS
    depth = jnp.concatenate([depth_ref[...], depth_ref[...]], axis=0)
    modes = jnp.concatenate(
        [modes[:half] + sign * modes[half:], modes_shared], axis=1
    )
    modes = jnp.where(within, modes, 0.0) / (1.0 + depth * ratio)
    updated = dot_split(halves(from_big), halves(modes[:, :WAVES]), AB)
    row_id = lax.broadcasted_iota(jnp.int32, updated.shape, 0)
    updated = jnp.where((row_id & FIELDS) == 0, updated, updated * sign)
    updated_shared = dot_split(halves(from_half), halves(modes[:, WAVES:]), AB)

    back = dot_split(halves(updated), (lh[:, :WAVES], ll[:, :WAVES]), ABT)
    back_shared = dot_split(halves(updated_shared), (lh[:, WAVES:], ll[:, WAVES:]), ABT)
    for start, part, values in ((0, PART, back), (MSG, 8, back_shared)):
        for u in range(ROWS // 2):
            row = start + 2 * u * part
            for g in range(0, FLD, 2):
                both = values[part * g : part * g + 2 * part, 128 * u : 128 * u + 128]
                one, two = both[:part], both[part:]
                for odd in range(2):
                    cut = slice(64 * odd, 64 * odd + 64)
                    y_ref[
                        row + part * odd : row + part * odd + part, LAT * g : LAT * g + 128
                    ] = jnp.concatenate([one[:, cut], two[:, cut]], axis=1)
    y_ref[MSG + HALF_MSG :, :] = jnp.zeros((LANES - MSG - HALF_MSG, LAT * FLD), F32)
    out_ref[...] = y_ref[...].T


def legendre_round(*args):
    smem = pl.BlockSpec(memory_space=pltpu.SMEM)
    vmem = pl.BlockSpec(memory_space=pltpu.VMEM)
    return pl.pallas_call(
        legendre_kernel,
        in_specs=[smem, smem] + [vmem] * 6,
        out_specs=vmem,
        out_shape=jax.ShapeDtypeStruct((LAT * FLD, LANES), F32),
        scratch_shapes=[
            pltpu.VMEM((PART * FLD, WAVES), F32),
            pltpu.VMEM((8 * FLD, WAVES), F32),
            pltpu.VMEM((LANES, LAT * FLD), F32),
        ],
        compiler_params=pltpu.CompilerParams(vmem_limit_bytes=VMEM),
        name="legendre_round",
    )(*args)


def body(grid, row_points, assignment, legendre, gauss_weights, to_modes, from_modes, mode_depths):
    waves = assignment.reshape(LAT, ROWS).T.reshape(1, WAVES).astype(F32)
    me = jnp.stack([lax.axis_index("fld"), lax.axis_index("lat")]).astype(jnp.int32)
    own, *messages = pack(me, legendre, gauss_weights)
    waves, own = lax.optimization_barrier((waves, own))
    rows, weight = unpack(me, own, ring(*messages))
    fourier = forward(row_points, waves, grid)
    coeffs = lax.all_to_all(fourier, ("fld", "lat"), 0, 0, tiled=True)
    depths = mode_depths.reshape(LEVELS, 1)
    synthesis = legendre_round(
        me, assignment, coeffs, to_modes, from_modes, depths, rows, weight
    )
    back = lax.all_to_all(synthesis, ("fld", "lat"), 0, 0, tiled=True)
    return inverse(row_points, waves, back)


def solution(mesh):
    placed = (
        P(None, "lat", "fld", None),
        P("lat"),
        P(),
        P("lat", "fld", None),
        P("fld"),
        P(),
        P(),
        P(),
    )
    return jax.shard_map(
        body, mesh=mesh, in_specs=placed, out_specs=P(None, "lat", "fld", None), check_vma=False
    )
```

```python
import math

import jax
import jax.numpy as jnp
from jax import lax
from jax.experimental import pallas as pl
from jax.experimental.pallas import tpu as pltpu
from jax.sharding import PartitionSpec as P

F32 = jnp.float32
BF16 = jnp.bfloat16

HEMI = 2
ROWS = 10
FIELDS = 4
LEVELS = 32
LON = 2688
BLOCKS = LON // 128
WAVES = 640
LAT = 64
FLD = 8
PART = 2 * HEMI * FIELDS
MSG = ROWS * PART
HALF_MSG = MSG // 2
LANES = 256
QUARTER = WAVES // 4
LEG = 896
BLOCK = FLD * ROWS
SLABS = 6
REST = SLABS * BLOCK
LMSG = REST + 24
TAIL = QUARTER - 128
WLANE = 64
FIRST = 256
VMEM = 20 << 20
ROUND_VMEM = 48 << 20
TRAVEL_COST = 5_000_000_000


def halves(x):
    top = x.astype(BF16)
    return top, (x - top.astype(F32)).astype(BF16)


def dot_split(a, b, dims):
    (ah, al), (bh, bl) = a, b
    d = (dims, ((), ()))
    out = lax.dot_general(ah, bl, d, preferred_element_type=F32)
    out = out + lax.dot_general(al, bh, d, preferred_element_type=F32)
    return out + lax.dot_general(ah, bh, d, preferred_element_type=F32)


AB = ((1,), (0,))
ABT = ((1,), (1,))


def turn(waves, points, index):
    product = waves * index
    quarter = points * 0.25
    count = jnp.floor(product * (4.0 / points) + 0.5)
    angle = (product - count * quarter) * (2.0 * math.pi / points)
    z = angle * angle
    s = angle * (
        1.0 + z * (-1 / 6 + z * (1 / 120 + z * (-1 / 5040 + z * (1 / 362880))))
    )
    c = 1.0 + z * (-0.5 + z * (1 / 24 + z * (-1 / 720 + z * (1 / 40320 - z / 3628800))))
    quad = count.astype(jnp.int32) & 3
    odd = (quad & 1) == 1
    cos_v = jnp.where(odd, s, c)
    sin_v = jnp.where(odd, c, s)
    cos_v = jnp.where((quad == 1) | (quad == 2), -cos_v, cos_v)
    sin_v = jnp.where(quad >= 2, -sin_v, sin_v)
    return cos_v, sin_v


def iota(shape, dim):
    return lax.broadcasted_iota(jnp.int32, shape, dim).astype(F32)


def tables(waves, points, cs_ref):
    c0, s0 = turn(waves, points, iota((16, WAVES), 0))
    c1, s1 = turn(waves, points, iota((8, WAVES), 0) * 16.0)
    for b in range(8):
        cb, sb = c1[b : b + 1], s1[b : b + 1]
        cs_ref[16 * b : 16 * b + 16, :WAVES] = c0 * cb - s0 * sb
        cs_ref[16 * b : 16 * b + 16, WAVES:] = s0 * cb + c0 * sb
    return turn(waves, points, iota((24, WAVES), 0) * 128.0)


def forward_kernel(points_ref, waves_ref, grid_ref, out_ref, cs_ref, fourier_ref):
    r = pl.program_id(0)
    count = points_ref[r]
    points = jnp.full((1, WAVES), count, jnp.int32).astype(F32)
    waves = waves_ref[...]
    co, so = tables(waves, points, cs_ref)
    wh, wl = halves(cs_ref[...])
    x = jnp.concatenate([grid_ref[0, 0], grid_ref[1, 0]], axis=0)
    column = lax.broadcasted_iota(jnp.int32, x.shape, 1)
    x = jnp.where(column < count, x, 0.0)
    x = jnp.concatenate([x[:, 128 * a : 128 * a + 128] for a in range(BLOCKS)], axis=0)
    xh, xl = halves(x)
    d = (AB, ((), ()))
    part = lax.dot_general(
        jnp.concatenate([xh, xl], axis=1),
        jnp.concatenate([wh, wh], axis=0),
        d,
        preferred_element_type=F32,
    ) + lax.dot_general(xh, wl, d, preferred_element_type=F32)
    re = jnp.zeros((8, WAVES), F32)
    im = jnp.zeros((8, WAVES), F32)
    for a in range(BLOCKS):
        pc = part[8 * a : 8 * a + 8, :WAVES]
        ps = part[8 * a : 8 * a + 8, WAVES:]
        ca, sa = co[a : a + 1], so[a : a + 1]
        re = re + (pc * ca - ps * sa)
        im = im - (ps * ca + pc * sa)
    scale = jnp.where(2.0 * waves < points, 1.0 / points, 0.0)
    row = pl.multiple_of(r * PART, PART)
    fourier_ref[pl.ds(row, 8), :] = re * scale
    fourier_ref[pl.ds(row + 8, 8), :] = im * scale

    @pl.when(r == ROWS - 1)
    def _():
        y = fourier_ref[...]
        top = lax.broadcasted_iota(jnp.int32, (8, 128), 0) < FIELDS
        low = lax.broadcasted_iota(jnp.int32, (8, 128), 1) < 64
        shared = []
        for row in range(0, MSG, PART):
            re, im = y[row : row + 8, 512:], y[row + 8 : row + PART, 512:]
            re_other, im_other = pltpu.roll(re, FIELDS, 0), pltpu.roll(im, FIELDS, 0)
            total = jnp.where(top, re + re_other, im + im_other)
            change = jnp.where(top, re - re_other, im_other - im)
            first = jnp.where(low, total, pltpu.roll(change, 64, 1))
            second = jnp.where(low, pltpu.roll(total, 64, 1), change)
            shared.append(jnp.concatenate([first, first, second, second], axis=1))
        pad = jnp.zeros((LANES - MSG - HALF_MSG, 512), F32)
        full = jnp.concatenate([y[:, :512], *shared, pad], axis=0)
        out_ref[...] = full.T


def forward(row_points, waves, grid):
    return pl.pallas_call(
        forward_kernel,
        grid=(ROWS,),
        in_specs=[
            pl.BlockSpec(memory_space=pltpu.SMEM),
            pl.BlockSpec((1, WAVES), lambda r: (0, 0)),
            pl.BlockSpec((HEMI, 1, FIELDS, LON), lambda r: (0, r, 0, 0)),
        ],
        out_specs=pl.BlockSpec((LAT * FLD, LANES), lambda r: (0, 0)),
        out_shape=jax.ShapeDtypeStruct((LAT * FLD, LANES), F32),
        scratch_shapes=[
            pltpu.VMEM((128, 2 * WAVES), F32),
            pltpu.VMEM((MSG, WAVES), F32),
        ],
        compiler_params=pltpu.CompilerParams(vmem_limit_bytes=VMEM),
        cost_estimate=pl.CostEstimate(
            flops=3_000_000_000, bytes_accessed=2_000_000, transcendentals=0
        ),
        name="forward_fourier",
    )(row_points, waves, grid)


def inverse_kernel(points_ref, waves_ref, coeff_ref, out_ref, cs_ref, fourier_ref):
    r = pl.program_id(0)

    @pl.when(r == 0)
    def _():
        t = coeff_ref[...].T
        fourier_ref[:, :512] = t[:MSG]
        top = lax.broadcasted_iota(jnp.int32, (8, 128), 0) < FIELDS
        low = lax.broadcasted_iota(jnp.int32, (8, 128), 1) < 64
        for i in range(ROWS):
            rows = slice(MSG + 8 * i, MSG + 8 * i + 8)
            one = t[rows, :128] + t[rows, 128:256]
            two = t[rows, 256:384] + t[rows, 384:]
            one_other, two_other = pltpu.roll(one, 64, 1), pltpu.roll(two, 64, 1)
            north = jnp.where(low, one + one_other, two + two_other)
            south = jnp.where(low, one - one_other, two_other - two)
            fourier_ref[PART * i : PART * i + 8, 512:] = jnp.where(
                top, north, pltpu.roll(south, FIELDS, 0)
            )
            fourier_ref[PART * i + 8 : PART * i + PART, 512:] = jnp.where(
                top, pltpu.roll(north, FIELDS, 0), south
            )

    count = points_ref[r]
    points = jnp.full((1, WAVES), count, jnp.int32).astype(F32)
    waves = waves_ref[...]
    co, so = tables(waves, points, cs_ref)
    wh, wl = halves(cs_ref[...])
    weight = jnp.where(2.0 * waves < points, jnp.where(waves == 0.0, 1.0, 2.0), 0.0)
    row = pl.multiple_of(r * PART, PART)
    re = fourier_ref[pl.ds(row, 8), :] * weight
    im = fourier_ref[pl.ds(row + 8, 8), :] * weight
    cosine, sine = [], []
    for a in range(BLOCKS):
        ca, sa = co[a : a + 1], so[a : a + 1]
        cosine.append(re * ca - im * sa)
        sine.append(-(re * sa + im * ca))
    turned = jnp.concatenate(
        [jnp.concatenate(cosine, axis=0), jnp.concatenate(sine, axis=0)], axis=1
    )
    th, tl = halves(turned)
    d = (ABT, ((), ()))
    both = lax.dot_general(
        th, jnp.concatenate([wh, wl], axis=0), d, preferred_element_type=F32
    )
    values = both[:, :128] + both[:, 128:]
    values = values + lax.dot_general(tl, wh, d, preferred_element_type=F32)
    wide = jnp.concatenate(
        [values[8 * a : 8 * a + 8] for a in range(BLOCKS)], axis=1
    )
    column = lax.broadcasted_iota(jnp.int32, wide.shape, 1)
    wide = jnp.where(column < count, wide, 0.0)
    out_ref[0, 0] = wide[:FIELDS]
    out_ref[1, 0] = wide[FIELDS:]


def inverse(row_points, waves, coeffs):
    return pl.pallas_call(
        inverse_kernel,
        grid=(ROWS,),
        in_specs=[
            pl.BlockSpec(memory_space=pltpu.SMEM),
            pl.BlockSpec((1, WAVES), lambda r: (0, 0)),
            pl.BlockSpec((LAT * FLD, LANES), lambda r: (0, 0)),
        ],
        out_specs=pl.BlockSpec((HEMI, 1, FIELDS, LON), lambda r: (0, r, 0, 0)),
        out_shape=jax.ShapeDtypeStruct((HEMI, ROWS, FIELDS, LON), F32),
        scratch_shapes=[
            pltpu.VMEM((128, 2 * WAVES), F32),
            pltpu.VMEM((MSG, WAVES), F32),
        ],
        compiler_params=pltpu.CompilerParams(vmem_limit_bytes=VMEM),
        name="inverse_fourier",
    )(row_points, waves, coeffs)


def quarter_degree(place):
    quarter = sum((place >= QUARTER * i).astype(jnp.int32) for i in range(1, 4))
    inside = place - QUARTER * quarter
    return 2 * (QUARTER * (quarter >> 1) + inside) + (quarter & 1)


def permuted(x, one_hot):
    out = None
    parts = []
    for _ in range(3):
        parts.append(x.astype(BF16))
        x = x - parts[-1].astype(F32)
    for part in reversed(parts):
        moved = lax.dot_general(part, one_hot, (AB, ((), ())), preferred_element_type=F32)
        out = moved if out is None else out + moved
    return out


def pack_kernel(me_ref, legendre_ref, weight_ref, *refs):
    near_refs = {0: refs[0], 1: refs[1], 7: refs[2]}
    up_ref, down_ref, tile_ref, order_ref = refs[3:]
    me = me_ref[0]
    lane = lax.broadcasted_iota(jnp.int32, (BLOCK, 128), 1)
    weight = jnp.concatenate(
        [weight_ref[:, ROWS * d : ROWS * d + ROWS] for d in range(FLD)], axis=0
    )
    weight = jnp.concatenate([weight, jnp.zeros((FLD, 128 - ROWS), F32)], axis=1)
    weight = pltpu.roll(weight, WLANE, 1)
    place = lax.broadcasted_iota(jnp.int32, (WAVES, WAVES), 1)
    degree = lax.broadcasted_iota(jnp.int32, (WAVES, WAVES), 0)
    one_hot = (degree == quarter_degree(place)).astype(BF16)
    for q in range(2):
        order_ref[q] = permuted(legendre_ref[FLD + q], one_hot)
    for t in range(FLD):

        def store(row, value, t=t):
            if t in (0, 1, 7):
                ref, at = near_refs[t], row
            elif t < 4:
                ref, at = up_ref, (t - 2) * LMSG + row
            elif t > 4:
                ref, at = down_ref, (6 - t) * LMSG + row
            elif row < FIRST:
                ref, at = up_ref, 2 * LMSG + row
            else:
                ref, at = down_ref, 2 * LMSG + row - FIRST
            ref[pl.ds(at, FLD), :] = value

        g = lax.rem(me + t, FLD)
        shift = lax.rem(WAVES - QUARTER * lax.rem(g, 4), WAVES)
        quarter = pltpu.roll(order_ref[g // 4], shift, 1)
        own = legendre_ref[g]
        for i in range(5):
            tile_ref[t, i] = own[:, 128 * i : 128 * i + 128]
        tile_ref[t, 5] = quarter[:, :128]
        tile_ref[t, 6] = jnp.where(lane < TAIL, quarter[:, 128:256], 0.0)
        for i in range(SLABS):
            for r in range(ROWS):
                rows = pl.ds(r, FLD, stride=ROWS)
                store(BLOCK * i + FLD * r, tile_ref[t, i, rows, :])
        for i in range(3):
            rest = weight if i == 2 else jnp.zeros((FLD, 128), F32)
            for r in range(4 * i, min(4 * i + 4, ROWS)):
                part = tile_ref[t, 6, pl.ds(r, FLD, stride=ROWS), :]
                rest = rest + (pltpu.roll(part, TAIL * (r % 4), 1) if r % 4 else part)
            store(REST + FLD * i, rest)


def pack(me, legendre, gauss_weights):
    vmem = pl.BlockSpec(memory_space=pltpu.VMEM)
    rows = (LMSG, LMSG, LMSG, 2 * LMSG + FIRST, 3 * LMSG - FIRST)
    return pl.pallas_call(
        pack_kernel,
        in_specs=[pl.BlockSpec(memory_space=pltpu.SMEM), vmem, vmem],
        out_specs=[vmem] * 5,
        out_shape=[jax.ShapeDtypeStruct((n, 128), F32) for n in rows],
        scratch_shapes=[
            pltpu.VMEM((FLD, LEG // 128, BLOCK, 128), F32),
            pltpu.VMEM((2, BLOCK, WAVES), F32),
        ],
        compiler_params=pltpu.CompilerParams(vmem_limit_bytes=VMEM),
        name="pack_legendre",
    )(me, legendre, gauss_weights.reshape(1, BLOCK))


def shift(x, step):
    return lax.ppermute(x, "fld", [(i, (i + step) % FLD) for i in range(FLD)])


def ring(up1, down1, up2, down2):
    up2, down2 = shift(up2, 2), shift(down2, -2)
    up1, down1 = shift(up1, 1), shift(down1, -1)
    up3, down3 = shift(up2[LMSG : 2 * LMSG], 1), shift(down2[LMSG : 2 * LMSG], -1)
    up4, down4 = shift(up2[2 * LMSG :], 2), shift(down2[2 * LMSG :], -2)
    return up1, up2, up3, up4, down1, down2, down3, down4


def mode_matrices(to_modes, from_modes):
    def ids(shape, dim):
        return lax.broadcasted_iota(jnp.int32, shape, dim)

    def product(a, b):
        return lax.dot_general(
            a, b, (AB, ((), ())), precision=lax.Precision.HIGHEST, preferred_element_type=F32
        )

    def field(part):
        return part // PART * FIELDS + part % FIELDS

    parts, modes = PART * FLD, 2 * LEVELS
    spread = (ids((LEVELS, parts), 0) == field(ids((LEVELS, parts), 1))).astype(F32)
    double = (ids((parts, LEVELS), 0) % LEVELS == ids((parts, LEVELS), 1)).astype(F32)
    wide = product(double, product(to_modes, spread))
    row, part = ids((parts, parts), 0), ids((parts, parts), 1) % PART
    to_big = jnp.where(
        (row // LEVELS % 2 == part // 8) & (row // modes == part % 8 // FIELDS), wide, 0.0
    )
    spread = (field(ids((parts, LEVELS), 0)) == ids((parts, LEVELS), 1)).astype(F32)
    double = (ids((LEVELS, modes), 0) == ids((LEVELS, modes), 1) % LEVELS).astype(F32)
    wide = product(product(spread, from_modes), double)
    part, column = ids((parts, modes), 0) % PART, ids((parts, modes), 1)
    from_big = jnp.where(part // 8 == column // LEVELS, wide, 0.0)

    def half_field(part):
        return part // 8 * FIELDS + part % FIELDS

    spread = (ids((LEVELS, modes), 0) == half_field(ids((LEVELS, modes), 1))).astype(F32)
    double = (ids((modes, LEVELS), 0) % LEVELS == ids((modes, LEVELS), 1)).astype(F32)
    wide = product(double, product(to_modes, spread))
    row, column = ids((modes, modes), 0), ids((modes, modes), 1)
    to_half = jnp.where(row // LEVELS == column % 8 // FIELDS, wide, 0.0)
    spread = (half_field(ids((modes, LEVELS), 0)) == ids((modes, LEVELS), 1)).astype(F32)
    double = (ids((LEVELS, modes), 0) == ids((LEVELS, modes), 1) % LEVELS).astype(F32)
    wide = product(product(spread, from_modes), double)
    from_half = jnp.where(row % 8 // FIELDS == column // LEVELS, wide, 0.0)
    return to_big, from_big, to_half, from_half


def unpack(fld, own_msg, ups, downs, leg_ref, weight_ref):
    lane = lax.broadcasted_iota(jnp.int32, (FLD, 128), 1)
    for t in range(FLD):

        def load(row, t=t):
            if t == 0:
                return own_msg[row : row + FLD]
            if t < 4:
                return ups[t - 1][row : row + FLD]
            if t > 4:
                return downs[7 - t][row : row + FLD]
            if row < FIRST:
                return ups[3][row : row + FLD]
            return downs[3][row - FIRST : row - FIRST + FLD]

        source = lax.rem(fld + FLD - t, FLD)
        for r in range(ROWS):
            place = pl.ds(pl.multiple_of(r * LAT + FLD * source, FLD), FLD)
            for i in range(SLABS):
                leg_ref[place, 128 * i : 128 * i + 128] = load(BLOCK * i + FLD * r)
            rest = load(REST + FLD * (r // 4))
            if r % 4:
                rest = pltpu.roll(rest, 128 - TAIL * (r % 4), 1)
            leg_ref[place, 768:] = jnp.where(lane < TAIL, rest, 0.0)
        weight_ref[pl.ds(pl.multiple_of(FLD * source, FLD), FLD), :] = load(REST + 2 * FLD)


def arrival_kernel(*refs):
    refs[-1][...] = jnp.zeros((8, 128), F32)


def arrival(moved):
    return pl.pallas_call(
        arrival_kernel,
        in_specs=[pl.BlockSpec(memory_space=pl.ANY)] * len(moved),
        out_specs=pl.BlockSpec(memory_space=pltpu.VMEM),
        out_shape=jax.ShapeDtypeStruct((8, 128), F32),
        compiler_params=pltpu.CompilerParams(vmem_limit_bytes=1 << 20),
        cost_estimate=pl.CostEstimate(
            flops=TRAVEL_COST, bytes_accessed=0, transcendentals=0
        ),
        name="arrival",
    )(*moved)


def legendre_kernel(
    me_ref, assignment_ref, coeff_ref, to_ref, from_ref, depth_ref, zero_ref, *refs
):
    own_msg, ups, downs = refs[0], refs[1:5], refs[5:9]
    out_ref, leg_ref, weight_ref, a_ref, x_ref, y_ref = refs[9:]
    lat, fld = me_ref[1], me_ref[0]
    unpack(fld, own_msg, ups, downs, leg_ref, weight_ref)
    weight = weight_ref[...].T
    weight = jnp.concatenate(
        [weight[WLANE + r : WLANE + r + 1] for r in range(ROWS)], axis=1
    )
    lh, ll = halves(leg_ref[...])

    t = coeff_ref[...].T
    for start, part, dest in ((0, PART, a_ref), (MSG, 8, x_ref)):
        for u in range(ROWS // 2):
            row = start + 2 * u * part
            even, odd = t[row : row + part], t[row + part : row + 2 * part]
            for g in range(FLD):
                cut = slice(LAT * g, LAT * g + LAT)
                dest[part * g : part * g + part, 128 * u : 128 * u + 128] = (
                    jnp.concatenate([even[:, cut], odd[:, cut]], axis=1)
                )
    own = halves(a_ref[...] * weight)
    shared = halves(x_ref[...] * weight)
    to_big, from_big, to_half, from_half = mode_matrices(to_ref[...], from_ref[...])
    spectrum = dot_split(own, (lh[:, :WAVES], ll[:, :WAVES]), AB)
    modes = dot_split(halves(to_big), halves(spectrum), AB)
    spectrum = dot_split(shared, (lh[:, WAVES:], ll[:, WAVES:]), AB)
    modes_shared = dot_split(halves(to_half), halves(spectrum), AB)

    lane = lax.broadcasted_iota(jnp.int32, (1, LEG), 1)
    is_own = lane < WAVES
    quarter = lax.rem(fld, 4)
    place = QUARTER * (quarter // 2) + lane - WAVES
    degree = jnp.where(is_own, lane, 2 * place + lax.rem(quarter, 2))
    wave_own = assignment_ref[lat * ROWS + fld]
    wave_shared = assignment_ref[lat * ROWS + FLD + fld // 4]
    total = degree + jnp.where(is_own, wave_own, wave_shared)
    within = (total < WAVES) & (lane < WAVES + QUARTER)
    total = jnp.where(within, total, 0)
    sign = jnp.where((degree & 1) == 0, 1.0, -1.0)[:, :WAVES]
    ratio = (total * (total + 1)).astype(F32) * (1.0 / (WAVES * (WAVES + 1)))
    half = 2 * LEVELS
    depth = jnp.concatenate([depth_ref[...], depth_ref[...]], axis=0)
    modes = jnp.concatenate(
        [modes[:half] + sign * modes[half:], modes_shared], axis=1
    )
    modes = jnp.where(within, modes, 0.0) / (1.0 + depth * ratio)
    updated = dot_split(halves(from_big), halves(modes[:, :WAVES]), AB)
    row_id = lax.broadcasted_iota(jnp.int32, updated.shape, 0)
    updated = jnp.where((row_id & FIELDS) == 0, updated, updated * sign)
    updated_shared = dot_split(halves(from_half), halves(modes[:, WAVES:]), AB)

    back = dot_split(halves(updated), (lh[:, :WAVES], ll[:, :WAVES]), ABT)
    back_shared = dot_split(halves(updated_shared), (lh[:, WAVES:], ll[:, WAVES:]), ABT)
    for start, part, values in ((0, PART, back), (MSG, 8, back_shared)):
        for u in range(ROWS // 2):
            row = start + 2 * u * part
            for g in range(0, FLD, 2):
                both = values[part * g : part * g + 2 * part, 128 * u : 128 * u + 128]
                one, two = both[:part], both[part:]
                for odd in range(2):
                    cut = slice(64 * odd, 64 * odd + 64)
                    y_ref[
                        row + part * odd : row + part * odd + part, LAT * g : LAT * g + 128
                    ] = jnp.concatenate([one[:, cut], two[:, cut]], axis=1)
    y_ref[MSG + HALF_MSG :, :] = jnp.zeros((LANES - MSG - HALF_MSG, LAT * FLD), F32)
    out_ref[...] = y_ref[...].T


def legendre_round(*args):
    smem = pl.BlockSpec(memory_space=pltpu.SMEM)
    vmem = pl.BlockSpec(memory_space=pltpu.VMEM)
    taken = [
        pl.BlockSpec((min(LMSG, x.shape[0]), 128), lambda i: (0, 0)) for x in args[8:]
    ]
    return pl.pallas_call(
        legendre_kernel,
        grid=(1,),
        in_specs=[smem, smem] + [vmem] * 6 + taken,
        out_specs=vmem,
        out_shape=jax.ShapeDtypeStruct((LAT * FLD, LANES), F32),
        scratch_shapes=[
            pltpu.VMEM((WAVES, LEG), F32),
            pltpu.VMEM((LAT, 128), F32),
            pltpu.VMEM((PART * FLD, WAVES), F32),
            pltpu.VMEM((8 * FLD, WAVES), F32),
            pltpu.VMEM((LANES, LAT * FLD), F32),
        ],
        compiler_params=pltpu.CompilerParams(vmem_limit_bytes=ROUND_VMEM),
        name="legendre_round",
    )(*args)


def body(grid, row_points, assignment, legendre, gauss_weights, to_modes, from_modes, mode_depths):
    waves = assignment.reshape(LAT, ROWS).T.reshape(1, WAVES).astype(F32)
    me = jnp.stack([lax.axis_index("fld"), lax.axis_index("lat")]).astype(jnp.int32)
    own, *messages = pack(me, legendre, gauss_weights)
    waves, own = lax.optimization_barrier((waves, own))
    moved = ring(*messages)
    zero = arrival(moved)
    fourier = forward(row_points, waves, grid)
    coeffs = lax.all_to_all(fourier, ("fld", "lat"), 0, 0, tiled=True)
    depths = mode_depths.reshape(LEVELS, 1)
    synthesis = legendre_round(
        me, assignment, coeffs, to_modes, from_modes, depths, zero, own, *moved
    )
    back = lax.all_to_all(synthesis, ("fld", "lat"), 0, 0, tiled=True)
    return inverse(row_points, waves, back)


def solution(mesh):
    placed = (
        P(None, "lat", "fld", None),
        P("lat"),
        P(),
        P("lat", "fld", None),
        P("fld"),
        P(),
        P(),
        P(),
    )
    return jax.shard_map(
        body, mesh=mesh, in_specs=placed, out_specs=P(None, "lat", "fld", None), check_vma=False
    )
```

```python
import math

import jax
import jax.numpy as jnp
from jax import lax
from jax.experimental import pallas as pl
from jax.experimental.pallas import tpu as pltpu
from jax.sharding import PartitionSpec as P

F32 = jnp.float32
BF16 = jnp.bfloat16

HEMI = 2
ROWS = 10
FIELDS = 4
LEVELS = 32
LON = 2688
BLOCKS = LON // 128
WAVES = 640
LAT = 64
FLD = 8
PART = 2 * HEMI * FIELDS
MSG = ROWS * PART
HALF_MSG = MSG // 2
LANES = 256
QUARTER = WAVES // 4
LEG = 896
BLOCK = FLD * ROWS
SLABS = 6
REST = SLABS * BLOCK
LMSG = REST + 24
TAIL = QUARTER - 128
WLANE = 64
FIRST = 256
VMEM = 20 << 20
ROUND_VMEM = 48 << 20
TRAVEL_COST = 5_000_000_000


def halves(x):
    top = x.astype(BF16)
    return top, (x - top.astype(F32)).astype(BF16)


def dot_split(a, b, dims):
    (ah, al), (bh, bl) = a, b
    d = (dims, ((), ()))
    out = lax.dot_general(ah, bl, d, preferred_element_type=F32)
    out = out + lax.dot_general(al, bh, d, preferred_element_type=F32)
    return out + lax.dot_general(ah, bh, d, preferred_element_type=F32)


AB = ((1,), (0,))
ABT = ((1,), (1,))


def turn(waves, points, index):
    product = waves * index
    quarter = points * 0.25
    count = jnp.floor(product * (4.0 / points) + 0.5)
    angle = (product - count * quarter) * (2.0 * math.pi / points)
    z = angle * angle
    s = angle * (
        1.0 + z * (-1 / 6 + z * (1 / 120 + z * (-1 / 5040 + z * (1 / 362880))))
    )
    c = 1.0 + z * (-0.5 + z * (1 / 24 + z * (-1 / 720 + z * (1 / 40320 - z / 3628800))))
    quad = count.astype(jnp.int32) & 3
    odd = (quad & 1) == 1
    cos_v = jnp.where(odd, s, c)
    sin_v = jnp.where(odd, c, s)
    cos_v = jnp.where((quad == 1) | (quad == 2), -cos_v, cos_v)
    sin_v = jnp.where(quad >= 2, -sin_v, sin_v)
    return cos_v, sin_v


def iota(shape, dim):
    return lax.broadcasted_iota(jnp.int32, shape, dim).astype(F32)


def tables(waves, points, cs_ref):
    c0, s0 = turn(waves, points, iota((16, WAVES), 0))
    c1, s1 = turn(waves, points, iota((8, WAVES), 0) * 16.0)
    for b in range(8):
        cb, sb = c1[b : b + 1], s1[b : b + 1]
        cs_ref[16 * b : 16 * b + 16, :WAVES] = c0 * cb - s0 * sb
        cs_ref[16 * b : 16 * b + 16, WAVES:] = s0 * cb + c0 * sb
    return turn(waves, points, iota((24, WAVES), 0) * 128.0)


def forward_kernel(points_ref, waves_ref, grid_ref, out_ref, cs_ref, fourier_ref):
    r = pl.program_id(0)
    count = points_ref[r]
    points = jnp.full((1, WAVES), count, jnp.int32).astype(F32)
    waves = waves_ref[...]
    co, so = tables(waves, points, cs_ref)
    wh, wl = halves(cs_ref[...])
    x = jnp.concatenate([grid_ref[0, 0], grid_ref[1, 0]], axis=0)
    column = lax.broadcasted_iota(jnp.int32, x.shape, 1)
    x = jnp.where(column < count, x, 0.0)
    x = jnp.concatenate([x[:, 128 * a : 128 * a + 128] for a in range(BLOCKS)], axis=0)
    xh, xl = halves(x)
    d = (AB, ((), ()))
    part = lax.dot_general(
        jnp.concatenate([xh, xl], axis=1),
        jnp.concatenate([wh, wh], axis=0),
        d,
        preferred_element_type=F32,
    ) + lax.dot_general(xh, wl, d, preferred_element_type=F32)
    re = jnp.zeros((8, WAVES), F32)
    im = jnp.zeros((8, WAVES), F32)
    for a in range(BLOCKS):
        pc = part[8 * a : 8 * a + 8, :WAVES]
        ps = part[8 * a : 8 * a + 8, WAVES:]
        ca, sa = co[a : a + 1], so[a : a + 1]
        re = re + (pc * ca - ps * sa)
        im = im - (ps * ca + pc * sa)
    scale = jnp.where(2.0 * waves < points, 1.0 / points, 0.0)
    row = pl.multiple_of(r * PART, PART)
    fourier_ref[pl.ds(row, 8), :] = re * scale
    fourier_ref[pl.ds(row + 8, 8), :] = im * scale

    @pl.when(r == ROWS - 1)
    def _():
        y = fourier_ref[...]
        top = lax.broadcasted_iota(jnp.int32, (8, 128), 0) < FIELDS
        low = lax.broadcasted_iota(jnp.int32, (8, 128), 1) < 64
        shared = []
        for row in range(0, MSG, PART):
            re, im = y[row : row + 8, 512:], y[row + 8 : row + PART, 512:]
            re_other, im_other = pltpu.roll(re, FIELDS, 0), pltpu.roll(im, FIELDS, 0)
            total = jnp.where(top, re + re_other, im + im_other)
            change = jnp.where(top, re - re_other, im_other - im)
            first = jnp.where(low, total, pltpu.roll(change, 64, 1))
            second = jnp.where(low, pltpu.roll(total, 64, 1), change)
            shared.append(jnp.concatenate([first, first, second, second], axis=1))
        pad = jnp.zeros((LANES - MSG - HALF_MSG, 512), F32)
        full = jnp.concatenate([y[:, :512], *shared, pad], axis=0)
        out_ref[...] = full.T


def forward(row_points, waves, grid):
    return pl.pallas_call(
        forward_kernel,
        grid=(ROWS,),
        in_specs=[
            pl.BlockSpec(memory_space=pltpu.SMEM),
            pl.BlockSpec((1, WAVES), lambda r: (0, 0)),
            pl.BlockSpec((HEMI, 1, FIELDS, LON), lambda r: (0, r, 0, 0)),
        ],
        out_specs=pl.BlockSpec((LAT * FLD, LANES), lambda r: (0, 0)),
        out_shape=jax.ShapeDtypeStruct((LAT * FLD, LANES), F32),
        scratch_shapes=[
            pltpu.VMEM((128, 2 * WAVES), F32),
            pltpu.VMEM((MSG, WAVES), F32),
        ],
        compiler_params=pltpu.CompilerParams(vmem_limit_bytes=VMEM),
        cost_estimate=pl.CostEstimate(
            flops=3_000_000_000, bytes_accessed=2_000_000, transcendentals=0
        ),
        name="forward_fourier",
    )(row_points, waves, grid)


def inverse_kernel(points_ref, waves_ref, coeff_ref, out_ref, cs_ref, fourier_ref):
    r = pl.program_id(0)

    @pl.when(r == 0)
    def _():
        t = coeff_ref[...].T
        fourier_ref[:, :512] = t[:MSG]
        top = lax.broadcasted_iota(jnp.int32, (8, 128), 0) < FIELDS
        low = lax.broadcasted_iota(jnp.int32, (8, 128), 1) < 64
        for i in range(ROWS):
            rows = slice(MSG + 8 * i, MSG + 8 * i + 8)
            one = t[rows, :128] + t[rows, 128:256]
            two = t[rows, 256:384] + t[rows, 384:]
            one_other, two_other = pltpu.roll(one, 64, 1), pltpu.roll(two, 64, 1)
            north = jnp.where(low, one + one_other, two + two_other)
            south = jnp.where(low, one - one_other, two_other - two)
            fourier_ref[PART * i : PART * i + 8, 512:] = jnp.where(
                top, north, pltpu.roll(south, FIELDS, 0)
            )
            fourier_ref[PART * i + 8 : PART * i + PART, 512:] = jnp.where(
                top, pltpu.roll(north, FIELDS, 0), south
            )

    count = points_ref[r]
    points = jnp.full((1, WAVES), count, jnp.int32).astype(F32)
    waves = waves_ref[...]
    co, so = tables(waves, points, cs_ref)
    wh, wl = halves(cs_ref[...])
    weight = jnp.where(2.0 * waves < points, jnp.where(waves == 0.0, 1.0, 2.0), 0.0)
    row = pl.multiple_of(r * PART, PART)
    re = fourier_ref[pl.ds(row, 8), :] * weight
    im = fourier_ref[pl.ds(row + 8, 8), :] * weight
    cosine, sine = [], []
    for a in range(BLOCKS):
        ca, sa = co[a : a + 1], so[a : a + 1]
        cosine.append(re * ca - im * sa)
        sine.append(-(re * sa + im * ca))
    turned = jnp.concatenate(
        [jnp.concatenate(cosine, axis=0), jnp.concatenate(sine, axis=0)], axis=1
    )
    th, tl = halves(turned)
    d = (ABT, ((), ()))
    both = lax.dot_general(
        th, jnp.concatenate([wh, wl], axis=0), d, preferred_element_type=F32
    )
    values = both[:, :128] + both[:, 128:]
    values = values + lax.dot_general(tl, wh, d, preferred_element_type=F32)
    wide = jnp.concatenate(
        [values[8 * a : 8 * a + 8] for a in range(BLOCKS)], axis=1
    )
    column = lax.broadcasted_iota(jnp.int32, wide.shape, 1)
    wide = jnp.where(column < count, wide, 0.0)
    out_ref[0, 0] = wide[:FIELDS]
    out_ref[1, 0] = wide[FIELDS:]


def inverse(row_points, waves, coeffs):
    return pl.pallas_call(
        inverse_kernel,
        grid=(ROWS,),
        in_specs=[
            pl.BlockSpec(memory_space=pltpu.SMEM),
            pl.BlockSpec((1, WAVES), lambda r: (0, 0)),
            pl.BlockSpec((LAT * FLD, LANES), lambda r: (0, 0)),
        ],
        out_specs=pl.BlockSpec((HEMI, 1, FIELDS, LON), lambda r: (0, r, 0, 0)),
        out_shape=jax.ShapeDtypeStruct((HEMI, ROWS, FIELDS, LON), F32),
        scratch_shapes=[
            pltpu.VMEM((128, 2 * WAVES), F32),
            pltpu.VMEM((MSG, WAVES), F32),
        ],
        compiler_params=pltpu.CompilerParams(vmem_limit_bytes=VMEM),
        name="inverse_fourier",
    )(row_points, waves, coeffs)


def quarter_degree(place):
    quarter = sum((place >= QUARTER * i).astype(jnp.int32) for i in range(1, 4))
    inside = place - QUARTER * quarter
    return 2 * (QUARTER * (quarter >> 1) + inside) + (quarter & 1)


def permuted(x, one_hot):
    out = None
    parts = []
    for _ in range(3):
        parts.append(x.astype(BF16))
        x = x - parts[-1].astype(F32)
    for part in reversed(parts):
        moved = lax.dot_general(part, one_hot, (AB, ((), ())), preferred_element_type=F32)
        out = moved if out is None else out + moved
    return out


def pack_kernel(me_ref, legendre_ref, weight_ref, *refs):
    near_refs = {0: refs[0], 1: refs[1], 7: refs[2]}
    up_ref, down_ref, tile_ref, order_ref = refs[3:]
    me = me_ref[0]
    lane = lax.broadcasted_iota(jnp.int32, (BLOCK, 128), 1)
    weight = jnp.concatenate(
        [weight_ref[:, ROWS * d : ROWS * d + ROWS] for d in range(FLD)], axis=0
    )
    weight = jnp.concatenate([weight, jnp.zeros((FLD, 128 - ROWS), F32)], axis=1)
    weight = pltpu.roll(weight, WLANE, 1)
    place = lax.broadcasted_iota(jnp.int32, (WAVES, WAVES), 1)
    degree = lax.broadcasted_iota(jnp.int32, (WAVES, WAVES), 0)
    one_hot = (degree == quarter_degree(place)).astype(BF16)
    for q in range(2):
        order_ref[q] = permuted(legendre_ref[FLD + q], one_hot)
    for t in range(FLD):

        def store(row, value, t=t):
            if t in (0, 1, 7):
                ref, at = near_refs[t], row
            elif t < 4:
                ref, at = up_ref, (t - 2) * LMSG + row
            elif t > 4:
                ref, at = down_ref, (6 - t) * LMSG + row
            elif row < FIRST:
                ref, at = up_ref, 2 * LMSG + row
            else:
                ref, at = down_ref, 2 * LMSG + row - FIRST
            ref[pl.ds(at, FLD), :] = value

        g = lax.rem(me + t, FLD)
        shift = lax.rem(WAVES - QUARTER * lax.rem(g, 4), WAVES)
        quarter = pltpu.roll(order_ref[g // 4], shift, 1)
        own = legendre_ref[g]
        for i in range(5):
            tile_ref[t, i] = own[:, 128 * i : 128 * i + 128]
        tile_ref[t, 5] = quarter[:, :128]
        tile_ref[t, 6] = jnp.where(lane < TAIL, quarter[:, 128:256], 0.0)
        for i in range(SLABS):
            for r in range(ROWS):
                rows = pl.ds(r, FLD, stride=ROWS)
                store(BLOCK * i + FLD * r, tile_ref[t, i, rows, :])
        for i in range(3):
            rest = weight if i == 2 else jnp.zeros((FLD, 128), F32)
            for r in range(4 * i, min(4 * i + 4, ROWS)):
                part = tile_ref[t, 6, pl.ds(r, FLD, stride=ROWS), :]
                rest = rest + (pltpu.roll(part, TAIL * (r % 4), 1) if r % 4 else part)
            store(REST + FLD * i, rest)


def pack(me, legendre, gauss_weights):
    vmem = pl.BlockSpec(memory_space=pltpu.VMEM)
    rows = (LMSG, LMSG, LMSG, 2 * LMSG + FIRST, 3 * LMSG - FIRST)
    return pl.pallas_call(
        pack_kernel,
        in_specs=[pl.BlockSpec(memory_space=pltpu.SMEM), vmem, vmem],
        out_specs=[vmem] * 5,
        out_shape=[jax.ShapeDtypeStruct((n, 128), F32) for n in rows],
        scratch_shapes=[
            pltpu.VMEM((FLD, LEG // 128, BLOCK, 128), F32),
            pltpu.VMEM((2, BLOCK, WAVES), F32),
        ],
        compiler_params=pltpu.CompilerParams(vmem_limit_bytes=VMEM),
        name="pack_legendre",
    )(me, legendre, gauss_weights.reshape(1, BLOCK))


def shift(x, step):
    return lax.ppermute(x, "fld", [(i, (i + step) % FLD) for i in range(FLD)])


def ring(up1, down1, up2, down2):
    far = shift(up2, 2), shift(down2, -2)
    third = (
        shift(jnp.concatenate([far[0][LMSG : 2 * LMSG], up1]), 1),
        shift(jnp.concatenate([far[1][LMSG : 2 * LMSG], down1]), -1),
    )
    fourth = shift(far[0][2 * LMSG :], 2), shift(far[1][2 * LMSG :], -2)
    return far, third, fourth


def mode_matrices(to_modes, from_modes):
    def ids(shape, dim):
        return lax.broadcasted_iota(jnp.int32, shape, dim)

    def product(a, b):
        return lax.dot_general(
            a, b, (AB, ((), ())), precision=lax.Precision.HIGHEST, preferred_element_type=F32
        )

    def field(part):
        return part // PART * FIELDS + part % FIELDS

    parts, modes = PART * FLD, 2 * LEVELS
    spread = (ids((LEVELS, parts), 0) == field(ids((LEVELS, parts), 1))).astype(F32)
    double = (ids((parts, LEVELS), 0) % LEVELS == ids((parts, LEVELS), 1)).astype(F32)
    wide = product(double, product(to_modes, spread))
    row, part = ids((parts, parts), 0), ids((parts, parts), 1) % PART
    to_big = jnp.where(
        (row // LEVELS % 2 == part // 8) & (row // modes == part % 8 // FIELDS), wide, 0.0
    )
    spread = (field(ids((parts, LEVELS), 0)) == ids((parts, LEVELS), 1)).astype(F32)
    double = (ids((LEVELS, modes), 0) == ids((LEVELS, modes), 1) % LEVELS).astype(F32)
    wide = product(product(spread, from_modes), double)
    part, column = ids((parts, modes), 0) % PART, ids((parts, modes), 1)
    from_big = jnp.where(part // 8 == column // LEVELS, wide, 0.0)

    def half_field(part):
        return part // 8 * FIELDS + part % FIELDS

    spread = (ids((LEVELS, modes), 0) == half_field(ids((LEVELS, modes), 1))).astype(F32)
    double = (ids((modes, LEVELS), 0) % LEVELS == ids((modes, LEVELS), 1)).astype(F32)
    wide = product(double, product(to_modes, spread))
    row, column = ids((modes, modes), 0), ids((modes, modes), 1)
    to_half = jnp.where(row // LEVELS == column % 8 // FIELDS, wide, 0.0)
    spread = (half_field(ids((modes, LEVELS), 0)) == ids((modes, LEVELS), 1)).astype(F32)
    double = (ids((LEVELS, modes), 0) == ids((LEVELS, modes), 1) % LEVELS).astype(F32)
    wide = product(product(spread, from_modes), double)
    from_half = jnp.where(row % 8 // FIELDS == column // LEVELS, wide, 0.0)
    return to_big, from_big, to_half, from_half


def unpack(fld, own_msg, ups, downs, leg_ref, weight_ref):
    lane = lax.broadcasted_iota(jnp.int32, (FLD, 128), 1)
    for t in range(FLD):

        def load(row, t=t):
            if t == 0:
                return own_msg[row : row + FLD]
            if t < 4:
                return ups[t - 1][row : row + FLD]
            if t > 4:
                return downs[7 - t][row : row + FLD]
            if row < FIRST:
                return ups[3][row : row + FLD]
            return downs[3][row - FIRST : row - FIRST + FLD]

        source = lax.rem(fld + FLD - t, FLD)
        for r in range(ROWS):
            place = pl.ds(pl.multiple_of(r * LAT + FLD * source, FLD), FLD)
            for i in range(SLABS):
                leg_ref[place, 128 * i : 128 * i + 128] = load(BLOCK * i + FLD * r)
            rest = load(REST + FLD * (r // 4))
            if r % 4:
                rest = pltpu.roll(rest, 128 - TAIL * (r % 4), 1)
            leg_ref[place, 768:] = jnp.where(lane < TAIL, rest, 0.0)
        weight_ref[pl.ds(pl.multiple_of(FLD * source, FLD), FLD), :] = load(REST + 2 * FLD)


def arrival_kernel(*refs):
    refs[-1][...] = jnp.zeros((8, 128), F32)


def arrival(moved):
    return pl.pallas_call(
        arrival_kernel,
        in_specs=[pl.BlockSpec(memory_space=pl.ANY)] * len(moved),
        out_specs=pl.BlockSpec(memory_space=pltpu.VMEM),
        out_shape=jax.ShapeDtypeStruct((8, 128), F32),
        compiler_params=pltpu.CompilerParams(vmem_limit_bytes=1 << 20),
        cost_estimate=pl.CostEstimate(
            flops=TRAVEL_COST, bytes_accessed=0, transcendentals=0
        ),
        name="arrival",
    )(*moved)


def legendre_kernel(
    me_ref, assignment_ref, coeff_ref, to_ref, from_ref, depth_ref, zero_ref, *refs
):
    own_msg, ups, downs = refs[0], refs[1:5], refs[5:9]
    out_ref, leg_ref, weight_ref, a_ref, x_ref, y_ref = refs[9:]
    lat, fld = me_ref[1], me_ref[0]
    unpack(fld, own_msg, ups, downs, leg_ref, weight_ref)
    weight = weight_ref[...].T
    weight = jnp.concatenate(
        [weight[WLANE + r : WLANE + r + 1] for r in range(ROWS)], axis=1
    )
    lh, ll = halves(leg_ref[...])

    t = coeff_ref[...].T
    for start, part, dest in ((0, PART, a_ref), (MSG, 8, x_ref)):
        for u in range(ROWS // 2):
            row = start + 2 * u * part
            even, odd = t[row : row + part], t[row + part : row + 2 * part]
            for g in range(FLD):
                cut = slice(LAT * g, LAT * g + LAT)
                dest[part * g : part * g + part, 128 * u : 128 * u + 128] = (
                    jnp.concatenate([even[:, cut], odd[:, cut]], axis=1)
                )
    own = halves(a_ref[...] * weight)
    shared = halves(x_ref[...] * weight)
    to_big, from_big, to_half, from_half = mode_matrices(to_ref[...], from_ref[...])
    spectrum = dot_split(own, (lh[:, :WAVES], ll[:, :WAVES]), AB)
    modes = dot_split(halves(to_big), halves(spectrum), AB)
    spectrum = dot_split(shared, (lh[:, WAVES:], ll[:, WAVES:]), AB)
    modes_shared = dot_split(halves(to_half), halves(spectrum), AB)

    lane = lax.broadcasted_iota(jnp.int32, (1, LEG), 1)
    is_own = lane < WAVES
    quarter = lax.rem(fld, 4)
    place = QUARTER * (quarter // 2) + lane - WAVES
    degree = jnp.where(is_own, lane, 2 * place + lax.rem(quarter, 2))
    wave_own = assignment_ref[lat * ROWS + fld]
    wave_shared = assignment_ref[lat * ROWS + FLD + fld // 4]
    total = degree + jnp.where(is_own, wave_own, wave_shared)
    within = (total < WAVES) & (lane < WAVES + QUARTER)
    total = jnp.where(within, total, 0)
    sign = jnp.where((degree & 1) == 0, 1.0, -1.0)[:, :WAVES]
    ratio = (total * (total + 1)).astype(F32) * (1.0 / (WAVES * (WAVES + 1)))
    half = 2 * LEVELS
    depth = jnp.concatenate([depth_ref[...], depth_ref[...]], axis=0)
    modes = jnp.concatenate(
        [modes[:half] + sign * modes[half:], modes_shared], axis=1
    )
    modes = jnp.where(within, modes, 0.0) / (1.0 + depth * ratio)
    updated = dot_split(halves(from_big), halves(modes[:, :WAVES]), AB)
    row_id = lax.broadcasted_iota(jnp.int32, updated.shape, 0)
    updated = jnp.where((row_id & FIELDS) == 0, updated, updated * sign)
    updated_shared = dot_split(halves(from_half), halves(modes[:, WAVES:]), AB)

    back = dot_split(halves(updated), (lh[:, :WAVES], ll[:, :WAVES]), ABT)
    back_shared = dot_split(halves(updated_shared), (lh[:, WAVES:], ll[:, WAVES:]), ABT)
    for start, part, values in ((0, PART, back), (MSG, 8, back_shared)):
        for u in range(ROWS // 2):
            row = start + 2 * u * part
            for g in range(0, FLD, 2):
                both = values[part * g : part * g + 2 * part, 128 * u : 128 * u + 128]
                one, two = both[:part], both[part:]
                for odd in range(2):
                    cut = slice(64 * odd, 64 * odd + 64)
                    y_ref[
                        row + part * odd : row + part * odd + part, LAT * g : LAT * g + 128
                    ] = jnp.concatenate([one[:, cut], two[:, cut]], axis=1)
    y_ref[MSG + HALF_MSG :, :] = jnp.zeros((LANES - MSG - HALF_MSG, LAT * FLD), F32)
    out_ref[...] = y_ref[...].T


def legendre_round(*args):
    smem = pl.BlockSpec(memory_space=pltpu.SMEM)
    vmem = pl.BlockSpec(memory_space=pltpu.VMEM)
    taken = [
        pl.BlockSpec((min(LMSG, x.shape[0]), 128), lambda i, place=place: (place, 0))
        for x, place in zip(args[8:], (1, 0, 0, 0) * 2)
    ]
    return pl.pallas_call(
        legendre_kernel,
        grid=(1,),
        in_specs=[smem, smem] + [vmem] * 6 + taken,
        out_specs=vmem,
        out_shape=jax.ShapeDtypeStruct((LAT * FLD, LANES), F32),
        scratch_shapes=[
            pltpu.VMEM((WAVES, LEG), F32),
            pltpu.VMEM((LAT, 128), F32),
            pltpu.VMEM((PART * FLD, WAVES), F32),
            pltpu.VMEM((8 * FLD, WAVES), F32),
            pltpu.VMEM((LANES, LAT * FLD), F32),
        ],
        compiler_params=pltpu.CompilerParams(vmem_limit_bytes=ROUND_VMEM),
        name="legendre_round",
    )(*args)


def body(grid, row_points, assignment, legendre, gauss_weights, to_modes, from_modes, mode_depths):
    waves = assignment.reshape(LAT, ROWS).T.reshape(1, WAVES).astype(F32)
    me = jnp.stack([lax.axis_index("fld"), lax.axis_index("lat")]).astype(jnp.int32)
    own, *messages = pack(me, legendre, gauss_weights)
    waves, own = lax.optimization_barrier((waves, own))
    far, third, fourth = ring(*messages)
    zero = arrival([*far, *third, *fourth])
    moved = [x for way in zip(third, far, third, fourth) for x in way]
    fourier = forward(row_points, waves, grid)
    coeffs = lax.all_to_all(fourier, ("fld", "lat"), 0, 0, tiled=True)
    depths = mode_depths.reshape(LEVELS, 1)
    synthesis = legendre_round(
        me, assignment, coeffs, to_modes, from_modes, depths, zero, own, *moved
    )
    back = lax.all_to_all(synthesis, ("fld", "lat"), 0, 0, tiled=True)
    return inverse(row_points, waves, back)


def solution(mesh):
    placed = (
        P(None, "lat", "fld", None),
        P("lat"),
        P(),
        P("lat", "fld", None),
        P("fld"),
        P(),
        P(),
        P(),
    )
    return jax.shard_map(
        body, mesh=mesh, in_specs=placed, out_specs=P(None, "lat", "fld", None), check_vma=False
    )
```

```python
import math

import jax
import jax.numpy as jnp
from jax import lax
from jax.experimental import pallas as pl
from jax.experimental.pallas import tpu as pltpu
from jax.sharding import PartitionSpec as P

F32 = jnp.float32
BF16 = jnp.bfloat16

HEMI = 2
ROWS = 10
FIELDS = 4
LEVELS = 32
LON = 2688
BLOCKS = LON // 128
WAVES = 640
LAT = 64
FLD = 8
PART = 2 * HEMI * FIELDS
MSG = ROWS * PART
HALF_MSG = MSG // 2
LANES = 256
QUARTER = WAVES // 4
LEG = 896
BLOCK = FLD * ROWS
SLABS = 6
REST = SLABS * BLOCK
LMSG = REST + 24
TAIL = QUARTER - 128
WLANE = 64
FIRST = 256
VMEM = 20 << 20
FORWARD_VMEM = 56 << 20
ROUND_VMEM = 48 << 20
TRAVEL_COST = 5_000_000_000


def halves(x):
    top = x.astype(BF16)
    return top, (x - top.astype(F32)).astype(BF16)


def dot_split(a, b, dims):
    (ah, al), (bh, bl) = a, b
    d = (dims, ((), ()))
    out = lax.dot_general(ah, bl, d, preferred_element_type=F32)
    out = out + lax.dot_general(al, bh, d, preferred_element_type=F32)
    return out + lax.dot_general(ah, bh, d, preferred_element_type=F32)


AB = ((1,), (0,))
ABT = ((1,), (1,))


def turn(waves, points, index):
    product = waves * index
    quarter = points * 0.25
    count = jnp.floor(product * (4.0 / points) + 0.5)
    angle = (product - count * quarter) * (2.0 * math.pi / points)
    z = angle * angle
    s = angle * (
        1.0 + z * (-1 / 6 + z * (1 / 120 + z * (-1 / 5040 + z * (1 / 362880))))
    )
    c = 1.0 + z * (-0.5 + z * (1 / 24 + z * (-1 / 720 + z * (1 / 40320 - z / 3628800))))
    quad = count.astype(jnp.int32) & 3
    odd = (quad & 1) == 1
    cos_v = jnp.where(odd, s, c)
    sin_v = jnp.where(odd, c, s)
    cos_v = jnp.where((quad == 1) | (quad == 2), -cos_v, cos_v)
    sin_v = jnp.where(quad >= 2, -sin_v, sin_v)
    return cos_v, sin_v


def iota(shape, dim):
    return lax.broadcasted_iota(jnp.int32, shape, dim).astype(F32)


def tables(waves, points, cs_ref):
    c0, s0 = turn(waves, points, iota((16, WAVES), 0))
    c1, s1 = turn(waves, points, iota((8, WAVES), 0) * 16.0)
    for b in range(8):
        cb, sb = c1[b : b + 1], s1[b : b + 1]
        cs_ref[16 * b : 16 * b + 16, :WAVES] = c0 * cb - s0 * sb
        cs_ref[16 * b : 16 * b + 16, WAVES:] = s0 * cb + c0 * sb
    return turn(waves, points, iota((24, WAVES), 0) * 128.0)


def forward_kernel(points_ref, waves_ref, grid_ref, out_ref, cs_ref, fourier_ref):
    r = pl.program_id(0)
    count = points_ref[r]
    points = jnp.full((1, WAVES), count, jnp.int32).astype(F32)
    waves = waves_ref[...]
    co, so = tables(waves, points, cs_ref)
    wh, wl = halves(cs_ref[...])
    x = jnp.concatenate([grid_ref[0, 0], grid_ref[1, 0]], axis=0)
    column = lax.broadcasted_iota(jnp.int32, x.shape, 1)
    x = jnp.where(column < count, x, 0.0)
    x = jnp.concatenate([x[:, 128 * a : 128 * a + 128] for a in range(BLOCKS)], axis=0)
    xh, xl = halves(x)
    d = (AB, ((), ()))
    part = lax.dot_general(
        jnp.concatenate([xh, xl], axis=1),
        jnp.concatenate([wh, wh], axis=0),
        d,
        preferred_element_type=F32,
    ) + lax.dot_general(xh, wl, d, preferred_element_type=F32)
    re = jnp.zeros((8, WAVES), F32)
    im = jnp.zeros((8, WAVES), F32)
    for a in range(BLOCKS):
        pc = part[8 * a : 8 * a + 8, :WAVES]
        ps = part[8 * a : 8 * a + 8, WAVES:]
        ca, sa = co[a : a + 1], so[a : a + 1]
        re = re + (pc * ca - ps * sa)
        im = im - (ps * ca + pc * sa)
    scale = jnp.where(2.0 * waves < points, 1.0 / points, 0.0)
    row = pl.multiple_of(r * PART, PART)
    fourier_ref[pl.ds(row, 8), :] = re * scale
    fourier_ref[pl.ds(row + 8, 8), :] = im * scale

    @pl.when(r == ROWS - 1)
    def _():
        y = fourier_ref[...]
        top = lax.broadcasted_iota(jnp.int32, (8, 128), 0) < FIELDS
        low = lax.broadcasted_iota(jnp.int32, (8, 128), 1) < 64
        shared = []
        for row in range(0, MSG, PART):
            re, im = y[row : row + 8, 512:], y[row + 8 : row + PART, 512:]
            re_other, im_other = pltpu.roll(re, FIELDS, 0), pltpu.roll(im, FIELDS, 0)
            total = jnp.where(top, re + re_other, im + im_other)
            change = jnp.where(top, re - re_other, im_other - im)
            first = jnp.where(low, total, pltpu.roll(change, 64, 1))
            second = jnp.where(low, pltpu.roll(total, 64, 1), change)
            shared.append(jnp.concatenate([first, first, second, second], axis=1))
        pad = jnp.zeros((LANES - MSG - HALF_MSG, 512), F32)
        full = jnp.concatenate([y[:, :512], *shared, pad], axis=0)
        out_ref[...] = full.T


def forward(row_points, waves, grid):
    return pl.pallas_call(
        forward_kernel,
        grid=(ROWS,),
        in_specs=[
            pl.BlockSpec(memory_space=pltpu.SMEM),
            pl.BlockSpec((1, WAVES), lambda r: (0, 0)),
            pl.BlockSpec((HEMI, 1, FIELDS, LON), lambda r: (0, r, 0, 0)),
        ],
        out_specs=pl.BlockSpec((LAT * FLD, LANES), lambda r: (0, 0)),
        out_shape=jax.ShapeDtypeStruct((LAT * FLD, LANES), F32),
        scratch_shapes=[
            pltpu.VMEM((128, 2 * WAVES), F32),
            pltpu.VMEM((MSG, WAVES), F32),
        ],
        compiler_params=pltpu.CompilerParams(vmem_limit_bytes=FORWARD_VMEM),
        cost_estimate=pl.CostEstimate(
            flops=3_000_000_000, bytes_accessed=2_000_000, transcendentals=0
        ),
        name="forward_fourier",
    )(row_points, waves, grid)


def inverse_kernel(points_ref, waves_ref, coeff_ref, out_ref, cs_ref, fourier_ref):
    r = pl.program_id(0)

    @pl.when(r == 0)
    def _():
        t = coeff_ref[...].T
        fourier_ref[:, :512] = t[:MSG]
        top = lax.broadcasted_iota(jnp.int32, (8, 128), 0) < FIELDS
        low = lax.broadcasted_iota(jnp.int32, (8, 128), 1) < 64
        for i in range(ROWS):
            rows = slice(MSG + 8 * i, MSG + 8 * i + 8)
            one = t[rows, :128] + t[rows, 128:256]
            two = t[rows, 256:384] + t[rows, 384:]
            one_other, two_other = pltpu.roll(one, 64, 1), pltpu.roll(two, 64, 1)
            north = jnp.where(low, one + one_other, two + two_other)
            south = jnp.where(low, one - one_other, two_other - two)
            fourier_ref[PART * i : PART * i + 8, 512:] = jnp.where(
                top, north, pltpu.roll(south, FIELDS, 0)
            )
            fourier_ref[PART * i + 8 : PART * i + PART, 512:] = jnp.where(
                top, pltpu.roll(north, FIELDS, 0), south
            )

    count = points_ref[r]
    points = jnp.full((1, WAVES), count, jnp.int32).astype(F32)
    waves = waves_ref[...]
    co, so = tables(waves, points, cs_ref)
    wh, wl = halves(cs_ref[...])
    weight = jnp.where(2.0 * waves < points, jnp.where(waves == 0.0, 1.0, 2.0), 0.0)
    row = pl.multiple_of(r * PART, PART)
    re = fourier_ref[pl.ds(row, 8), :] * weight
    im = fourier_ref[pl.ds(row + 8, 8), :] * weight
    cosine, sine = [], []
    for a in range(BLOCKS):
        ca, sa = co[a : a + 1], so[a : a + 1]
        cosine.append(re * ca - im * sa)
        sine.append(-(re * sa + im * ca))
    turned = jnp.concatenate(
        [jnp.concatenate(cosine, axis=0), jnp.concatenate(sine, axis=0)], axis=1
    )
    th, tl = halves(turned)
    d = (ABT, ((), ()))
    both = lax.dot_general(
        th, jnp.concatenate([wh, wl], axis=0), d, preferred_element_type=F32
    )
    values = both[:, :128] + both[:, 128:]
    values = values + lax.dot_general(tl, wh, d, preferred_element_type=F32)
    wide = jnp.concatenate(
        [values[8 * a : 8 * a + 8] for a in range(BLOCKS)], axis=1
    )
    column = lax.broadcasted_iota(jnp.int32, wide.shape, 1)
    wide = jnp.where(column < count, wide, 0.0)
    out_ref[0, 0] = wide[:FIELDS]
    out_ref[1, 0] = wide[FIELDS:]


def inverse(row_points, waves, coeffs):
    return pl.pallas_call(
        inverse_kernel,
        grid=(ROWS,),
        in_specs=[
            pl.BlockSpec(memory_space=pltpu.SMEM),
            pl.BlockSpec((1, WAVES), lambda r: (0, 0)),
            pl.BlockSpec((LAT * FLD, LANES), lambda r: (0, 0)),
        ],
        out_specs=pl.BlockSpec((HEMI, 1, FIELDS, LON), lambda r: (0, r, 0, 0)),
        out_shape=jax.ShapeDtypeStruct((HEMI, ROWS, FIELDS, LON), F32),
        scratch_shapes=[
            pltpu.VMEM((128, 2 * WAVES), F32),
            pltpu.VMEM((MSG, WAVES), F32),
        ],
        compiler_params=pltpu.CompilerParams(vmem_limit_bytes=VMEM),
        name="inverse_fourier",
    )(row_points, waves, coeffs)


def quarter_degree(place):
    quarter = sum((place >= QUARTER * i).astype(jnp.int32) for i in range(1, 4))
    inside = place - QUARTER * quarter
    return 2 * (QUARTER * (quarter >> 1) + inside) + (quarter & 1)


def permuted(x, one_hot):
    out = None
    parts = []
    for _ in range(3):
        parts.append(x.astype(BF16))
        x = x - parts[-1].astype(F32)
    for part in reversed(parts):
        moved = lax.dot_general(part, one_hot, (AB, ((), ())), preferred_element_type=F32)
        out = moved if out is None else out + moved
    return out


def pack_kernel(me_ref, legendre_ref, weight_ref, *refs):
    near_refs = {0: refs[0], 1: refs[1], 7: refs[2]}
    up_ref, down_ref, tile_ref, order_ref = refs[3:]
    me = me_ref[0]
    lane = lax.broadcasted_iota(jnp.int32, (BLOCK, 128), 1)
    weight = jnp.concatenate(
        [weight_ref[:, ROWS * d : ROWS * d + ROWS] for d in range(FLD)], axis=0
    )
    weight = jnp.concatenate([weight, jnp.zeros((FLD, 128 - ROWS), F32)], axis=1)
    weight = pltpu.roll(weight, WLANE, 1)
    place = lax.broadcasted_iota(jnp.int32, (WAVES, WAVES), 1)
    degree = lax.broadcasted_iota(jnp.int32, (WAVES, WAVES), 0)
    one_hot = (degree == quarter_degree(place)).astype(BF16)
    for q in range(2):
        order_ref[q] = permuted(legendre_ref[FLD + q], one_hot)
    for t in range(FLD):

        def store(row, value, t=t):
            if t in (0, 1, 7):
                ref, at = near_refs[t], row
            elif t < 4:
                ref, at = up_ref, (t - 2) * LMSG + row
            elif t > 4:
                ref, at = down_ref, (6 - t) * LMSG + row
            elif row < FIRST:
                ref, at = up_ref, 2 * LMSG + row
            else:
                ref, at = down_ref, 2 * LMSG + row - FIRST
            ref[pl.ds(at, FLD), :] = value

        g = lax.rem(me + t, FLD)
        shift = lax.rem(WAVES - QUARTER * lax.rem(g, 4), WAVES)
        quarter = pltpu.roll(order_ref[g // 4], shift, 1)
        own = legendre_ref[g]
        for i in range(5):
            tile_ref[t, i] = own[:, 128 * i : 128 * i + 128]
        tile_ref[t, 5] = quarter[:, :128]
        tile_ref[t, 6] = jnp.where(lane < TAIL, quarter[:, 128:256], 0.0)
        for i in range(SLABS):
            for r in range(ROWS):
                rows = pl.ds(r, FLD, stride=ROWS)
                store(BLOCK * i + FLD * r, tile_ref[t, i, rows, :])
        for i in range(3):
            rest = weight if i == 2 else jnp.zeros((FLD, 128), F32)
            for r in range(4 * i, min(4 * i + 4, ROWS)):
                part = tile_ref[t, 6, pl.ds(r, FLD, stride=ROWS), :]
                rest = rest + (pltpu.roll(part, TAIL * (r % 4), 1) if r % 4 else part)
            store(REST + FLD * i, rest)


def pack(me, legendre, gauss_weights):
    vmem = pl.BlockSpec(memory_space=pltpu.VMEM)
    rows = (LMSG, LMSG, LMSG, 2 * LMSG + FIRST, 3 * LMSG - FIRST)
    return pl.pallas_call(
        pack_kernel,
        in_specs=[pl.BlockSpec(memory_space=pltpu.SMEM), vmem, vmem],
        out_specs=[vmem] * 5,
        out_shape=[jax.ShapeDtypeStruct((n, 128), F32) for n in rows],
        scratch_shapes=[
            pltpu.VMEM((FLD, LEG // 128, BLOCK, 128), F32),
            pltpu.VMEM((2, BLOCK, WAVES), F32),
        ],
        compiler_params=pltpu.CompilerParams(vmem_limit_bytes=VMEM),
        name="pack_legendre",
    )(me, legendre, gauss_weights.reshape(1, BLOCK))


def shift(x, step):
    return lax.ppermute(x, "fld", [(i, (i + step) % FLD) for i in range(FLD)])


def ring(up1, down1, up2, down2):
    far = shift(up2, 2), shift(down2, -2)
    third = (
        shift(jnp.concatenate([far[0][LMSG : 2 * LMSG], up1]), 1),
        shift(jnp.concatenate([far[1][LMSG : 2 * LMSG], down1]), -1),
    )
    fourth = shift(far[0][2 * LMSG :], 2), shift(far[1][2 * LMSG :], -2)
    return far, third, fourth


def mode_matrices(to_modes, from_modes):
    def ids(shape, dim):
        return lax.broadcasted_iota(jnp.int32, shape, dim)

    def product(a, b):
        return lax.dot_general(
            a, b, (AB, ((), ())), precision=lax.Precision.HIGHEST, preferred_element_type=F32
        )

    def field(part):
        return part // PART * FIELDS + part % FIELDS

    parts, modes = PART * FLD, 2 * LEVELS
    spread = (ids((LEVELS, parts), 0) == field(ids((LEVELS, parts), 1))).astype(F32)
    double = (ids((parts, LEVELS), 0) % LEVELS == ids((parts, LEVELS), 1)).astype(F32)
    wide = product(double, product(to_modes, spread))
    row, part = ids((parts, parts), 0), ids((parts, parts), 1) % PART
    to_big = jnp.where(
        (row // LEVELS % 2 == part // 8) & (row // modes == part % 8 // FIELDS), wide, 0.0
    )
    spread = (field(ids((parts, LEVELS), 0)) == ids((parts, LEVELS), 1)).astype(F32)
    double = (ids((LEVELS, modes), 0) == ids((LEVELS, modes), 1) % LEVELS).astype(F32)
    wide = product(product(spread, from_modes), double)
    part, column = ids((parts, modes), 0) % PART, ids((parts, modes), 1)
    from_big = jnp.where(part // 8 == column // LEVELS, wide, 0.0)

    def half_field(part):
        return part // 8 * FIELDS + part % FIELDS

    spread = (ids((LEVELS, modes), 0) == half_field(ids((LEVELS, modes), 1))).astype(F32)
    double = (ids((modes, LEVELS), 0) % LEVELS == ids((modes, LEVELS), 1)).astype(F32)
    wide = product(double, product(to_modes, spread))
    row, column = ids((modes, modes), 0), ids((modes, modes), 1)
    to_half = jnp.where(row // LEVELS == column % 8 // FIELDS, wide, 0.0)
    spread = (half_field(ids((modes, LEVELS), 0)) == ids((modes, LEVELS), 1)).astype(F32)
    double = (ids((LEVELS, modes), 0) == ids((LEVELS, modes), 1) % LEVELS).astype(F32)
    wide = product(product(spread, from_modes), double)
    from_half = jnp.where(row % 8 // FIELDS == column // LEVELS, wide, 0.0)
    return to_big, from_big, to_half, from_half


def unpack(fld, own_msg, ups, downs, leg_ref, weight_ref):
    lane = lax.broadcasted_iota(jnp.int32, (FLD, 128), 1)
    for t in range(FLD):

        def load(row, t=t):
            if t == 0:
                return own_msg[row : row + FLD]
            if t < 4:
                return ups[t - 1][row : row + FLD]
            if t > 4:
                return downs[7 - t][row : row + FLD]
            if row < FIRST:
                return ups[3][row : row + FLD]
            return downs[3][row - FIRST : row - FIRST + FLD]

        source = lax.rem(fld + FLD - t, FLD)
        for r in range(ROWS):
            place = pl.ds(pl.multiple_of(r * LAT + FLD * source, FLD), FLD)
            for i in range(SLABS):
                leg_ref[place, 128 * i : 128 * i + 128] = load(BLOCK * i + FLD * r)
            rest = load(REST + FLD * (r // 4))
            if r % 4:
                rest = pltpu.roll(rest, 128 - TAIL * (r % 4), 1)
            leg_ref[place, 768:] = jnp.where(lane < TAIL, rest, 0.0)
        weight_ref[pl.ds(pl.multiple_of(FLD * source, FLD), FLD), :] = load(REST + 2 * FLD)


def arrival_kernel(*refs):
    refs[-1][...] = jnp.zeros((8, 128), F32)


def arrival(moved):
    return pl.pallas_call(
        arrival_kernel,
        in_specs=[pl.BlockSpec(memory_space=pl.ANY)] * len(moved),
        out_specs=pl.BlockSpec(memory_space=pltpu.VMEM),
        out_shape=jax.ShapeDtypeStruct((8, 128), F32),
        compiler_params=pltpu.CompilerParams(vmem_limit_bytes=1 << 20),
        cost_estimate=pl.CostEstimate(
            flops=TRAVEL_COST, bytes_accessed=0, transcendentals=0
        ),
        name="arrival",
    )(*moved)


def legendre_kernel(
    me_ref, assignment_ref, coeff_ref, to_ref, from_ref, depth_ref, zero_ref, *refs
):
    own_msg, ups, downs = refs[0], refs[1:5], refs[5:9]
    out_ref, leg_ref, weight_ref, a_ref, x_ref, y_ref = refs[9:]
    lat, fld = me_ref[1], me_ref[0]
    unpack(fld, own_msg, ups, downs, leg_ref, weight_ref)
    weight = weight_ref[...].T
    weight = jnp.concatenate(
        [weight[WLANE + r : WLANE + r + 1] for r in range(ROWS)], axis=1
    )
    lh, ll = halves(leg_ref[...])

    t = coeff_ref[...].T
    for start, part, dest in ((0, PART, a_ref), (MSG, 8, x_ref)):
        for u in range(ROWS // 2):
            row = start + 2 * u * part
            even, odd = t[row : row + part], t[row + part : row + 2 * part]
            for g in range(FLD):
                cut = slice(LAT * g, LAT * g + LAT)
                dest[part * g : part * g + part, 128 * u : 128 * u + 128] = (
                    jnp.concatenate([even[:, cut], odd[:, cut]], axis=1)
                )
    own = halves(a_ref[...] * weight)
    shared = halves(x_ref[...] * weight)
    to_big, from_big, to_half, from_half = mode_matrices(to_ref[...], from_ref[...])
    spectrum = dot_split(own, (lh[:, :WAVES], ll[:, :WAVES]), AB)
    modes = dot_split(halves(to_big), halves(spectrum), AB)
    spectrum = dot_split(shared, (lh[:, WAVES:], ll[:, WAVES:]), AB)
    modes_shared = dot_split(halves(to_half), halves(spectrum), AB)

    lane = lax.broadcasted_iota(jnp.int32, (1, LEG), 1)
    is_own = lane < WAVES
    quarter = lax.rem(fld, 4)
    place = QUARTER * (quarter // 2) + lane - WAVES
    degree = jnp.where(is_own, lane, 2 * place + lax.rem(quarter, 2))
    wave_own = assignment_ref[lat * ROWS + fld]
    wave_shared = assignment_ref[lat * ROWS + FLD + fld // 4]
    total = degree + jnp.where(is_own, wave_own, wave_shared)
    within = (total < WAVES) & (lane < WAVES + QUARTER)
    total = jnp.where(within, total, 0)
    sign = jnp.where((degree & 1) == 0, 1.0, -1.0)[:, :WAVES]
    ratio = (total * (total + 1)).astype(F32) * (1.0 / (WAVES * (WAVES + 1)))
    half = 2 * LEVELS
    depth = jnp.concatenate([depth_ref[...], depth_ref[...]], axis=0)
    modes = jnp.concatenate(
        [modes[:half] + sign * modes[half:], modes_shared], axis=1
    )
    modes = jnp.where(within, modes, 0.0) / (1.0 + depth * ratio)
    updated = dot_split(halves(from_big), halves(modes[:, :WAVES]), AB)
    row_id = lax.broadcasted_iota(jnp.int32, updated.shape, 0)
    updated = jnp.where((row_id & FIELDS) == 0, updated, updated * sign)
    updated_shared = dot_split(halves(from_half), halves(modes[:, WAVES:]), AB)

    back = dot_split(halves(updated), (lh[:, :WAVES], ll[:, :WAVES]), ABT)
    back_shared = dot_split(halves(updated_shared), (lh[:, WAVES:], ll[:, WAVES:]), ABT)
    for start, part, values in ((0, PART, back), (MSG, 8, back_shared)):
        for u in range(ROWS // 2):
            row = start + 2 * u * part
            for g in range(0, FLD, 2):
                both = values[part * g : part * g + 2 * part, 128 * u : 128 * u + 128]
                one, two = both[:part], both[part:]
                for odd in range(2):
                    cut = slice(64 * odd, 64 * odd + 64)
                    y_ref[
                        row + part * odd : row + part * odd + part, LAT * g : LAT * g + 128
                    ] = jnp.concatenate([one[:, cut], two[:, cut]], axis=1)
    y_ref[MSG + HALF_MSG :, :] = jnp.zeros((LANES - MSG - HALF_MSG, LAT * FLD), F32)
    out_ref[...] = y_ref[...].T


def legendre_round(*args):
    smem = pl.BlockSpec(memory_space=pltpu.SMEM)
    vmem = pl.BlockSpec(memory_space=pltpu.VMEM)
    taken = [
        pl.BlockSpec((min(LMSG, x.shape[0]), 128), lambda i, place=place: (place, 0))
        for x, place in zip(args[8:], (1, 0, 0, 0) * 2)
    ]
    return pl.pallas_call(
        legendre_kernel,
        grid=(1,),
        in_specs=[smem, smem] + [vmem] * 6 + taken,
        out_specs=vmem,
        out_shape=jax.ShapeDtypeStruct((LAT * FLD, LANES), F32),
        scratch_shapes=[
            pltpu.VMEM((WAVES, LEG), F32),
            pltpu.VMEM((LAT, 128), F32),
            pltpu.VMEM((PART * FLD, WAVES), F32),
            pltpu.VMEM((8 * FLD, WAVES), F32),
            pltpu.VMEM((LANES, LAT * FLD), F32),
        ],
        compiler_params=pltpu.CompilerParams(vmem_limit_bytes=ROUND_VMEM),
        name="legendre_round",
    )(*args)


def body(grid, row_points, assignment, legendre, gauss_weights, to_modes, from_modes, mode_depths):
    waves = assignment.reshape(LAT, ROWS).T.reshape(1, WAVES).astype(F32)
    me = jnp.stack([lax.axis_index("fld"), lax.axis_index("lat")]).astype(jnp.int32)
    own, *messages = pack(me, legendre, gauss_weights)
    waves, own = lax.optimization_barrier((waves, own))
    far, third, fourth = ring(*messages)
    zero = arrival([*far, *third, *fourth])
    moved = [x for way in zip(third, far, third, fourth) for x in way]
    fourier = forward(row_points, waves, grid)
    coeffs = lax.all_to_all(fourier, ("fld", "lat"), 0, 0, tiled=True)
    depths = mode_depths.reshape(LEVELS, 1)
    synthesis = legendre_round(
        me, assignment, coeffs, to_modes, from_modes, depths, zero, own, *moved
    )
    back = lax.all_to_all(synthesis, ("fld", "lat"), 0, 0, tiled=True)
    return inverse(row_points, waves, back)


def solution(mesh):
    placed = (
        P(None, "lat", "fld", None),
        P("lat"),
        P(),
        P("lat", "fld", None),
        P("fld"),
        P(),
        P(),
        P(),
    )
    return jax.shard_map(
        body, mesh=mesh, in_specs=placed, out_specs=P(None, "lat", "fld", None), check_vma=False
    )
```
